256 devices in a mesh: comp: 4 (over z_hi, core), lon: 16 (over y, z_lo), lat: 4 (over x).
Axes of the slice: x: 4, y: 4, z: 8 (z_hi: 2, z_lo: 4; z = z_hi * 4 + z_lo), core: 2. Of those that a mesh axis runs over, the one named last changes fastest.
Arguments:
- shell: float32 [8, 32, 1024, 512], P(None, None, ('comp', 'lon'), 'lat'), may hold values from -6 to 6
- resistivity: float32 [32, 1024, 512], P(None, ('comp', 'lon'), 'lat'), may hold values from 0.02 to 0.2
- jacobians: float32 [3, 8, 8], replicated, may hold values from -2 to 2
- current_weights: float32 [8], replicated, may hold values from -4 to 4
- footpoint: int32 [4, 1024, 1], P('lat', ('comp', 'lon')), may hold values from 0 to 15; in each aligned block of 16 rows (0 to 15, 16 to 31, ..., all dimensions but the last counted through in order) at most 2 rows name the same one
- footrow: int32 [4, 1024], P('lat', ('comp', 'lon')), may hold values from 0 to 15
- slab: float32 [40, 8, 1024, 512], P(None, None, ('comp', 'lon'), 'lat'), may hold values from -6 to 6
- conductance: float32 [1024, 512], P(('comp', 'lon'), 'lat'), may hold values from 0.5 to 2
- chemistry: float32 [40, 40], replicated, may hold values from -1 to 1
- coupling: float32 [40, 8], replicated, may hold values from -4 to 4
- potential_weights: float32 [40], replicated, may hold values from -1 to 1
Outputs:
- shell_next: float32 [8, 32, 1024, 512], P(None, None, ('comp', 'lon'), 'lat')
- slab_next: float32 [40, 8, 1024, 512], P(None, None, ('comp', 'lon'), 'lat')
- boundary_potential: float32 [1024, 512], P(('comp', 'lon'), 'lat')
The draws below stay inside these ranges and needn't reach their ends.
Inputs may be any that keep to these rules, and one draw needn't show every extreme that they name: `footpoint`: within the 16 rows of one device, no value is named by more than 2 rows.
All inputs are finite; a program needn't handle non-finite values.
Results may differ from the reference program's by a relative error of at most 0.00007.
Values sent between devices are 32-bit elements; how exact they have to be, the bound alone decides.
No kernel may reach another device: no remote copies, remote signals or barrier semaphores. Data moves between devices by JAX's collectives and lax.ppermute only.
A program may use at most 128 MiB of HBM per device.

```python
import math
import jax
import jax.numpy as jnp
import numpy as np
from jax import lax

NV = 8
NF = 40
R_DEV = 32
PH_DEV = 16
TH_DEV = 128
LON_A = 16
LEV = 8
CAP = 2
NPH = 1024
NTH = 512
NLON = 1024
N_LON = 16
N_LAT = 4


def plant(result, key, low, largest):
    spot = [jax.random.randint(jax.random.fold_in(key, axis), (), 0, length) for axis, length in enumerate(result.shape)]
    longest = result.shape.index(max(result.shape))
    next_to = spot[:longest] + [(spot[longest] + 1) % result.shape[longest]] + spot[longest + 1:]
    return result.at[tuple(spot)].set(low).at[tuple(next_to)].set(largest)


def block_levels(rng, shape, shards, least, largest):
    def one(position, blocks):
        draws = jax.random.uniform(jax.random.fold_in(jax.random.fold_in(rng, 6), position), (blocks,), jnp.float32, least / len(shards), largest / len(shards))
        return jnp.repeat(jnp.exp(draws), shape[position] // blocks).reshape((-1,) + (1,) * (len(shape) - position - 1))

    loudness = one(*shards[0])
    for cut in shards[1:]:
        loudness = loudness * one(*cut)
    return loudness


def shared_out(key, own, number, rows, count, top, bound, lean):
    sequence = jax.random.permutation(key, count)
    heavy_load, ordinary = portions_of(count, rows * top, bound, lean, True), portions_of(count, rows * top, bound, lean, False)
    places = jnp.arange(count)

    def named(sizes, turn):
        used = int((sizes > 0).sum())
        fixed = max(1, used // 4)
        moved = fixed + (places - fixed + turn * (used - fixed)) % max(1, count - fixed)
        return jnp.zeros((count,), jnp.int32).at[sequence[jnp.where(places < fixed, places, moved)]].set(jnp.asarray(sizes, jnp.int32))

    sizes = jnp.where(number % 4 == 0, named(heavy_load, number // 4), named(ordinary, number - number // 4 - 1))
    mixed = jax.random.permutation(jax.random.fold_in(own, 3), count)
    source_of, sink = mixed[0:count // 2 * 2:2], mixed[1:count // 2 * 2:2]
    margin = jnp.minimum(sizes[source_of] - 1, bound - sizes[sink]) // 2
    margin = jnp.where((source_of == sequence[0]) | (sink == sequence[0]) | (sizes[sink] == 0), 0, jnp.maximum(margin, 0))
    moved = jax.random.randint(jax.random.fold_in(own, 4), (count // 2,), 0, 1 << 20) % (margin + 1)
    sizes = sizes.at[source_of].add(-moved).at[sink].add(moved)
    members = jnp.searchsorted(jnp.cumsum(sizes), jnp.arange(rows * top), side="right").astype(jnp.int32)
    grid = members.reshape(top, rows).T
    grid = grid[jax.random.permutation(jax.random.fold_in(own, 1), rows)]
    turn = jax.random.randint(jax.random.fold_in(own, 2), (rows, 1), 0, top)
    return jnp.take_along_axis(grid, (jnp.arange(top)[None, :] + turn) % top, axis=1)


def portions_of(count, total, most, slope, full):
    portions = [(1 << 20) // math.isqrt(grade ** slope) + 1 for grade in range(1, count + 1)]
    largest = most if full else min(most, max(-(-total // count), total * portions[0] // sum(portions)))
    least = 1 if total - largest >= count - 1 else 0
    counts, surplus = [largest] + [least] * (count - 1), total - largest - least * (count - 1)
    while surplus > 0:
        movable = [i for i in range(1, count) if counts[i] < largest] or [i for i in range(1, count) if counts[i] < most]
        mass, remaining = sum([portions[i] for i in movable]), surplus
        for i in movable:
            more = min(most - counts[i], max(1, remaining * portions[i] // mass), surplus)
            counts[i] = counts[i] + more
            surplus = surplus - more
    return np.array(counts)


def bell_draw(stream_key, extent, deviation, most, cuts=(), kind=jnp.bfloat16):
    values = jax.random.normal(stream_key, extent, jnp.float32) * deviation
    if len(cuts) > 0:
        values = block_levels(stream_key, extent, cuts, -0.22, 0.18) * values
    return jnp.clip(values, min=-most, max=most).astype(kind)


def setup_inputs(seed: int = 0) -> dict:
    splits = jax.random.split(jax.random.key(seed), 12)
    shell = bell_draw(splits[0], (NV, R_DEV, NPH, NTH), 1.0, 6.0, ((2, 64), (3, 4)), jnp.float32)
    resistivity = jnp.clip(jnp.exp(math.log(0.2) - 2.3025851 * jax.random.uniform(splits[1], (R_DEV, NPH, NTH), jnp.float32) ** block_levels(splits[1], (R_DEV, NPH, NTH), ((1, 64), (2, 4)), -0.2, 0.2)), 0.02, 0.2)
    jacobians = bell_draw(splits[2], (3, NV, NV), NV ** -0.5, 2.0, (), jnp.float32)
    current_weights = bell_draw(splits[3], (NV,), 1.0, 4.0, (), jnp.float32)
    footpoint_keys = jax.random.split(jax.random.fold_in(splits[4], 1), N_LAT * NPH // PH_DEV)
    footpoint_turns = jax.random.permutation(jax.random.fold_in(splits[4], 3), N_LAT * NPH // PH_DEV)
    footpoint = jax.vmap(lambda own, number: shared_out(jax.random.fold_in(splits[4], 2), own, number, PH_DEV, N_LON, 1, CAP, 2))(footpoint_keys, footpoint_turns).reshape((N_LAT, NPH, 1))
    footrow = plant(jax.random.randint(splits[5], (N_LAT, NPH), 0, LON_A), jax.random.fold_in(splits[5], 1), 0, LON_A - 1).astype(jnp.int32)
    slab = bell_draw(splits[6], (NF, LEV, NLON, NTH), 1.0, 6.0, ((2, 64), (3, 4)), jnp.float32)
    conductance = jnp.clip(jnp.exp(math.log(2.0) - 1.3862944 * jax.random.uniform(splits[7], (NLON, NTH), jnp.float32) ** block_levels(splits[7], (NLON, NTH), ((0, 64), (1, 4)), -0.2, 0.2)), 0.5, 2.0)
    chemistry = bell_draw(splits[8], (NF, NF), NF ** -0.5, 1.0, (), jnp.float32)
    coupling = bell_draw(splits[9], (NF, LEV), 1.0, 4.0, (), jnp.float32)
    potential_weights = bell_draw(splits[10], (NF,), NF ** -0.5, 1.0, (), jnp.float32)
    return dict(shell=shell, resistivity=resistivity, jacobians=jacobians, current_weights=current_weights, footpoint=footpoint, footrow=footrow, slab=slab, conductance=conductance, chemistry=chemistry, coupling=coupling, potential_weights=potential_weights)


STEP = 0.2
HORIZ = 0.1
VERTICAL = 0.1
COUPLE = 0.1


def shell_update(state, extended, resist, jacobians):
    padded = jnp.pad(state, ((0, 0), (1, 1), (0, 0), (0, 0)))
    d_radial = 0.5 * (padded[:, 2:] - padded[:, :-2])
    d_azimuth = 0.5 * (extended[:, :, 2:, 1:-1] - extended[:, :, :-2, 1:-1])
    d_polar = 0.5 * (extended[:, :, 1:-1, 2:] - extended[:, :, 1:-1, :-2])
    laplace = padded[:, 2:] + padded[:, :-2] + extended[:, :, 2:, 1:-1] + extended[:, :, :-2, 1:-1]
    laplace = laplace + extended[:, :, 1:-1, 2:] + extended[:, :, 1:-1, :-2] - 6.0 * state
    flux = jnp.einsum('uv,vrpt->urpt', jacobians[0], d_radial, precision=lax.Precision.HIGHEST)
    flux = flux + jnp.einsum('uv,vrpt->urpt', jacobians[1], d_azimuth, precision=lax.Precision.HIGHEST)
    flux = flux + jnp.einsum('uv,vrpt->urpt', jacobians[2], d_polar, precision=lax.Precision.HIGHEST)
    return state + STEP * (resist[None] * laplace - flux)


def slab_update(fields, extended, conductance, chemistry, coupling, source):
    horizontal = extended[:, :, 2:, 1:-1] + extended[:, :, :-2, 1:-1] + extended[:, :, 1:-1, 2:] + extended[:, :, 1:-1, :-2] - 4.0 * fields
    padded = jnp.pad(fields, ((0, 0), (1, 1), (0, 0), (0, 0)))
    vertical = padded[:, 2:] + padded[:, :-2] - 2.0 * fields
    mixing = jnp.einsum('fg,gklt->fklt', chemistry, fields, precision=lax.Precision.HIGHEST)
    forcing = coupling[:, :, None, None] * source[None, None]
    return fields + HORIZ * conductance[None, None] * horizontal + VERTICAL * vertical + COUPLE * (mixing + forcing)


def wrap_extend(array):
    wrapped = jnp.concatenate([array[:, :, -1:], array, array[:, :, :1]], axis=2)
    return jnp.pad(wrapped, ((0, 0), (0, 0), (0, 0), (1, 1)))


def reference(shell, resistivity, jacobians, current_weights, footpoint, footrow, slab, conductance, chemistry, coupling, potential_weights):
    shell_next = shell_update(shell, wrap_extend(shell), resistivity, jacobians)
    currents = jnp.einsum('v,vpt->pt', current_weights, shell_next[:, 0], precision=lax.Precision.HIGHEST)
    rows_all = currents.reshape(NPH, N_LAT, TH_DEV).transpose(1, 0, 2)
    azimuth = jnp.arange(NPH, dtype=jnp.int32)
    group = azimuth // (N_LON * PH_DEV)
    owner = (group[None, :] * N_LON + footpoint[:, :, 0]) * LON_A + footrow
    band = jnp.broadcast_to(jnp.arange(N_LAT, dtype=jnp.int32)[:, None], owner.shape)
    placed = jnp.zeros((N_LAT, NLON, TH_DEV), jnp.float32).at[band, owner].add(rows_all)
    source = placed.transpose(1, 0, 2).reshape(NLON, NTH)
    slab_mid = slab_update(slab, wrap_extend(slab), conductance, chemistry, coupling, source)
    slab_next = slab_update(slab_mid, wrap_extend(slab_mid), conductance, chemistry, coupling, source)
    potential = jnp.einsum('f,flt->lt', potential_weights, slab_next[:, 0], precision=lax.Precision.HIGHEST)
    split_rows = potential.reshape(NLON, N_LAT, TH_DEV)
    picked = split_rows[owner, band]
    boundary_potential = picked.transpose(1, 0, 2).reshape(NPH, NTH)
    return shell_next, slab_next, boundary_potential
```

```python
import functools

import jax
import jax.numpy as jnp
from jax import lax
from jax.experimental import pallas as pl
from jax.experimental.pallas import tpu as pltpu
from jax.sharding import PartitionSpec as P

NV = 8
NF = 40
RAD = 32
PH = 16
TH = 128
LEV = 8
LON = 16
BLOCKS = 16
KF = LEV * NF
SHELL_ROWS = NV * RAD
F32 = jnp.float32
BF16 = jnp.bfloat16
VMEM = pl.BlockSpec(memory_space=pltpu.VMEM)
SMEM = pl.BlockSpec(memory_space=pltpu.SMEM)
PARAMS = pltpu.CompilerParams(vmem_limit_bytes=48 * 1024 * 1024)


def odd_lon():
    return lax.rem(lax.axis_index("lon"), 2) == 1


def odd_lat():
    return lax.rem(lax.axis_index("lat"), 2) == 1


def lanes(rows):
    return lax.broadcasted_iota(jnp.int32, (rows, TH), 1)


def slot_of(rows):
    return lax.rem(lanes(rows) + 1, TH) // 2


def edge_of(rows):
    lane = lanes(rows)
    return (lane == 0) | (lane == TH - 1)


def spin(x, shift):
    shift = shift % TH
    return x if shift == 0 else pltpu.roll(x, shift, 1)


def merged(first, second):
    odd = odd_lat()
    left = jnp.where(odd, first, second)
    right = jnp.where(odd, second, first)
    even_lane = lax.rem(lanes(left.shape[0]), 2) == 0
    return jnp.where(even_lane, spin(left, 1), spin(right, -1))


def pack_kernel(slab_ref, shell_ref, s2_ref, lon_a_ref, lon_b_ref, lat_ref):
    slot = slot_of(NF)
    for half in range(2):
        acc = jnp.zeros((NF, TH), F32)
        for k in range(half * 4, half * 4 + 4):
            for l in range(LON):
                x = slab_ref[pl.ds(k * LON + l, NF, stride=LEV * LON), :]
                s2_ref[l, k * NF : (k + 1) * NF, :] = x
                j = l + LON * (k % 4)
                acc = jnp.where(slot == j, spin(x, 2 * j), acc)
        lat_ref[half * NF : (half + 1) * NF, :] = acc
    slot = slot_of(PH)
    for v in range(NV):
        acc = jnp.zeros((PH, TH), F32)
        for r in range(RAD):
            x = shell_ref[(v * RAD + r) * PH : (v * RAD + r + 1) * PH, :]
            acc = jnp.where(slot == r, spin(x, 2 * r), acc)
        lat_ref[2 * NF + v * PH : 2 * NF + (v + 1) * PH, :] = acc
    odd = odd_lon()
    low, high = s2_ref[0], s2_ref[LON - 1]
    lon_a_ref[0:KF, :] = jnp.where(odd, low, high)
    lon_b_ref[0:KF, :] = jnp.where(odd, high, low)
    for v in range(NV):
        low = shell_ref[pl.ds(v * RAD * PH, RAD, stride=PH), :]
        high = shell_ref[pl.ds(v * RAD * PH + PH - 1, RAD, stride=PH), :]
        at = KF + v * RAD
        lon_a_ref[at : at + RAD, :] = jnp.where(odd, low, high)
        lon_b_ref[at : at + RAD, :] = jnp.where(odd, high, low)


def mixing_matrix(chem):
    rows = (lax.broadcasted_iota(jnp.int32, (2 * NF, NF), 0) % NF) == lax.broadcasted_iota(
        jnp.int32, (2 * NF, NF), 1
    )
    cols = lax.broadcasted_iota(jnp.int32, (NF, 6 * NF), 0) == (
        lax.broadcasted_iota(jnp.int32, (NF, 6 * NF), 1) % NF
    )
    wide = jnp.dot(
        jnp.dot(
            rows.astype(F32), chem, precision=lax.Precision.HIGHEST, preferred_element_type=F32
        ),
        cols.astype(F32),
        precision=lax.Precision.HIGHEST,
        preferred_element_type=F32,
    )
    i = lax.broadcasted_iota(jnp.int32, (2 * NF, 6 * NF), 0)
    j = lax.broadcasted_iota(jnp.int32, (2 * NF, 6 * NF), 1)
    wide = jnp.where((i // NF) == ((j // NF) % 2), 0.1 * wide, 0.0)
    high = wide.astype(BF16).astype(F32)
    return jnp.where(j < 4 * NF, high, wide - high).astype(BF16)


def step_kernel(x_ref, cond_ref, chem_ref, o_ref):
    lhs = mixing_matrix(chem_ref[...])
    lane = lanes(2 * NF)
    zero = jnp.zeros((NF, TH), F32)

    def body(g, carry):
        for kp in range(LEV // 2):
            rows = slice(2 * NF * kp, 2 * NF * (kp + 1))
            xs = [x_ref[2 * g, rows, :], x_ref[2 * g + 1, rows, :]]
            below = x_ref[jnp.maximum(2 * g - 1, 0), rows, :] * jnp.where(g > 0, 1.0, 0.0)
            above = x_ref[jnp.minimum(2 * g + 2, LON - 1), rows, :] * jnp.where(
                g < LON // 2 - 1, 1.0, 0.0
            )
            near = [below + xs[1], xs[0] + above]
            both = jnp.concatenate(xs, axis=1)
            high = both.astype(BF16)
            low = (both - high.astype(F32)).astype(BF16)
            mixed = jnp.dot(
                lhs, jnp.concatenate([high, low, high], axis=0), preferred_element_type=F32
            )
            for i in range(2):
                x = xs[i]
                l = 2 * g + i
                if kp == 0:
                    down = jnp.concatenate([zero, x[:NF]], axis=0)
                else:
                    down = x_ref[l, 2 * NF * kp - NF : 2 * NF * kp + NF, :]
                if kp == LEV // 2 - 1:
                    up = jnp.concatenate([x[NF:], zero], axis=0)
                else:
                    up = x_ref[l, 2 * NF * kp + NF : 2 * NF * kp + 3 * NF, :]
                sides = jnp.where(lane == 0, 0.0, spin(x, 1)) + jnp.where(
                    lane == TH - 1, 0.0, spin(x, -1)
                )
                c = 0.1 * cond_ref[pl.ds(l, 1), :]
                o_ref[l, rows, :] = (
                    x * (0.8 - 4.0 * c)
                    + c * (near[i] + sides)
                    + 0.1 * (up + down)
                    + mixed[:, i * TH : (i + 1) * TH]
                )
        return carry

    lax.fori_loop(0, LON // 2, body, 0)


def shell_kernel(x_ref, res_ref, jac_ref, o_ref):
    lane = lanes(PH)
    row = lax.broadcasted_iota(jnp.int32, (PH, TH), 0)

    def body(r, carry):
        keep_low = jnp.where(r > 0, 1.0, 0.0)
        keep_high = jnp.where(r < RAD - 1, 1.0, 0.0)
        flux = [None] * NV
        for v in range(NV):
            x = x_ref[v, r]
            below = x_ref[v, jnp.maximum(r - 1, 0)] * keep_low
            above = x_ref[v, jnp.minimum(r + 1, RAD - 1)] * keep_high
            west = jnp.where(row == 0, 0.0, pltpu.roll(x, 1, 0))
            east = jnp.where(row == PH - 1, 0.0, pltpu.roll(x, PH - 1, 0))
            south = jnp.where(lane == 0, 0.0, spin(x, 1))
            north = jnp.where(lane == TH - 1, 0.0, spin(x, -1))
            around = (below + above) + (west + east) + (south + north)
            o_ref[v, r] = x + (0.2 * res_ref[r]) * (around - 6.0 * x)
            parts = (above - below, east - west, north - south)
            for u in range(NV):
                for d in range(3):
                    term = jac_ref[d, u, v] * parts[d]
                    flux[u] = term if flux[u] is None else flux[u] + term
        for u in range(NV):
            o_ref[u, r] = o_ref[u, r] - 0.1 * flux[u]
        return carry

    lax.fori_loop(0, RAD, body, 0)


def rank_rows(fp_ref, count_ref, visit):
    for b in range(BLOCKS):
        count_ref[b] = 0
    for p in range(PH):
        block = fp_ref[0, p, 0]
        rank = count_ref[block]
        count_ref[block] = rank + 1
        visit(p, block, rank)


def current_kernel(
    part_ref, res_ref, jac_ref, weight_ref, fp_ref, row_ref, lon_a_ref, lon_b_ref, lat_a_ref, lat_b_ref,
    send_ref, cur_ref, count_ref,
):
    w = [weight_ref[v] for v in range(NV)]
    wj = [[sum(w[u] * jac_ref[d, u, v] for u in range(NV)) for v in range(NV)] for d in (1, 2)]
    res = 0.2 * res_ref[0]
    odd = odd_lon()
    cur = sum(w[v] * part_ref[v, 0] for v in range(NV))
    rows_a = [lon_a_ref[KF + v * RAD : KF + v * RAD + 1, :] for v in range(NV)]
    rows_b = [lon_b_ref[KF + v * RAD : KF + v * RAD + 1, :] for v in range(NV)]
    low = [jnp.where(odd, a, b) for a, b in zip(rows_a, rows_b)]
    high = [jnp.where(odd, b, a) for a, b in zip(rows_a, rows_b)]
    row = lax.broadcasted_iota(jnp.int32, (PH, TH), 0)
    lane = lanes(PH)
    plain = sum(w[v] * low[v] for v in range(NV))
    turned = 0.1 * sum(wj[0][v] * low[v] for v in range(NV))
    cur = cur + jnp.where(row == 0, res * plain + turned, 0.0)
    plain = sum(w[v] * high[v] for v in range(NV))
    turned = 0.1 * sum(wj[0][v] * high[v] for v in range(NV))
    cur = cur + jnp.where(row == PH - 1, res * plain - turned, 0.0)
    side = [
        merged(
            lat_a_ref[2 * NF + v * PH : 2 * NF + (v + 1) * PH, :],
            lat_b_ref[2 * NF + v * PH : 2 * NF + (v + 1) * PH, :],
        )
        for v in range(NV)
    ]
    plain = sum(w[v] * side[v] for v in range(NV))
    turned = 0.1 * sum(wj[1][v] * side[v] for v in range(NV))
    cur = cur + jnp.where(lane == 0, res * plain + turned, 0.0)
    cur = cur + jnp.where(lane == TH - 1, res * plain - turned, 0.0)
    cur_ref[...] = cur
    send_ref[...] = jnp.zeros(send_ref.shape, F32)

    def visit(p, block, rank):
        send_ref[block, pl.ds(rank, 1), :] = cur_ref[p : p + 1, :]
        send_ref[block, pl.ds(2 + rank, 1), :] = jnp.full((1, TH), row_ref[0, p], jnp.int32).astype(F32)

    rank_rows(fp_ref, count_ref, visit)


def slab_edges(lat_a, lat_b):
    return [
        merged(lat_a[h * NF : (h + 1) * NF, :], lat_b[h * NF : (h + 1) * NF, :]) for h in range(2)
    ]


def levels_of(coupling_ref):
    return [
        jnp.broadcast_to(0.1 * coupling_ref[:, k : k + 1], (NF, TH)) for k in range(LEV)
    ]


def gather_source(got_ref):
    row = lax.broadcasted_iota(jnp.int32, (LON, TH), 0).astype(F32)
    source = jnp.zeros((LON, TH), F32)
    for b in range(BLOCKS):
        for s in range(2):
            source = source + jnp.where(
                row == got_ref[b, 2 + s : 3 + s, :], got_ref[b, s : s + 1, :], 0.0
            )
    return source


def fixed_tile(x_ref, l, k, c, edge, sides, levels, source, ends):
    rows = slice(k * NF, (k + 1) * NF)
    j = l + LON * (k % 4)
    h = jnp.where(edge, spin(sides[k // 4], -2 * j), 0.0)
    if l == 0:
        h = h + ends[0][rows]
    if l == LON - 1:
        h = h + ends[1][rows]
    return x_ref[l, rows, :] + c * h + levels[k] * source


def middle_kernel(
    x_ref, lon_a_ref, lon_b_ref, lat_a_ref, lat_b_ref, cond_ref, coupling_ref, got_ref,
    o_ref, source_ref, next_a_ref, next_b_ref, lat_ref,
):
    source = gather_source(got_ref)
    source_ref[...] = source
    odd = odd_lon()
    ends = [
        jnp.where(odd, lon_a_ref[0:KF, :], lon_b_ref[0:KF, :]),
        jnp.where(odd, lon_b_ref[0:KF, :], lon_a_ref[0:KF, :]),
    ]
    sides = slab_edges(lat_a_ref, lat_b_ref)
    levels = levels_of(coupling_ref)
    edge = edge_of(NF)
    slot = slot_of(NF)
    for half in range(2):
        acc = jnp.zeros((NF, TH), F32)
        for l in range(LON):
            c = 0.1 * cond_ref[l : l + 1, :]
            for k in range(half * 4, half * 4 + 4):
                x = fixed_tile(x_ref, l, k, c, edge, sides, levels, source_ref[l : l + 1, :], ends)
                o_ref[l, k * NF : (k + 1) * NF, :] = x
                j = l + LON * (k % 4)
                acc = jnp.where(slot == j, spin(x, 2 * j), acc)
        lat_ref[half * NF : (half + 1) * NF, :] = acc
    low, high = o_ref[0], o_ref[LON - 1]
    next_a_ref[...] = jnp.where(odd, low, high)
    next_b_ref[...] = jnp.where(odd, high, low)


def ends_of(lon_a_ref, lon_b_ref, rows):
    odd = odd_lon()
    a, b = lon_a_ref[0:rows, :], lon_b_ref[0:rows, :]
    return [jnp.where(odd, a, b), jnp.where(odd, b, a)]


def potential_kernel(
    x_ref, lon_a_ref, lon_b_ref, lat_a_ref, lat_b_ref, cond_ref, coupling_ref, weight_ref, source_ref, got_ref,
    send_ref, pot_ref,
):
    ends = ends_of(lon_a_ref, lon_b_ref, NF)
    sides = [merged(lat_a_ref[0:NF, :], lat_b_ref[0:NF, :])]
    levels = [jnp.broadcast_to(0.1 * coupling_ref[:, 0:1], (NF, TH))]
    edge = edge_of(NF)
    diagonal = lax.broadcasted_iota(jnp.int32, (NF, NF), 0) == lax.broadcasted_iota(
        jnp.int32, (NF, NF), 1
    )
    weight = jnp.sum(
        jnp.where(diagonal, jnp.broadcast_to(weight_ref[...], (NF, NF)), 0.0), axis=1, keepdims=True
    )
    weight = jnp.broadcast_to(weight, (NF, TH))
    for l in range(LON):
        c = 0.1 * cond_ref[l : l + 1, :]
        x = fixed_tile(x_ref, l, 0, c, edge, sides, levels, source_ref[l : l + 1, :], ends)
        pot_ref[l : l + 1, :] = jnp.sum(weight * x, axis=0, keepdims=True)
    potential = pot_ref[...]
    row = lax.broadcasted_iota(jnp.int32, (LON, TH), 0).astype(F32)
    for b in range(BLOCKS):
        for s in range(2):
            send_ref[b, s : s + 1, :] = jnp.sum(
                jnp.where(row == got_ref[b, 2 + s : 3 + s, :], potential, 0.0), axis=0, keepdims=True
            )
        send_ref[b, 2:8, :] = jnp.zeros((6, TH), F32)


def finish_kernel(
    x_ref, lon_a_ref, lon_b_ref, lat_a_ref, lat_b_ref, cond_ref, coupling_ref, source_ref, o_ref
):
    ends = ends_of(lon_a_ref, lon_b_ref, KF)
    sides = slab_edges(lat_a_ref, lat_b_ref)
    levels = levels_of(coupling_ref)
    edge = edge_of(NF)
    for l in range(LON):
        c = 0.1 * cond_ref[l : l + 1, :]
        for k in range(LEV):
            o_ref[pl.ds(k * LON + l, NF, stride=LEV * LON), :] = fixed_tile(
                x_ref, l, k, c, edge, sides, levels, source_ref[l : l + 1, :], ends
            )


def shell_edge_kernel(
    part_ref, res_ref, jac_ref, lon_a_ref, lon_b_ref, lat_a_ref, lat_b_ref, o_ref, corr_ref
):
    odd = odd_lon()
    slot = slot_of(PH)
    edge = edge_of(PH)
    even_lane = lax.rem(lanes(PH), 2) == 0
    packed = jnp.zeros((PH, TH), F32)
    for r in range(RAD):
        packed = jnp.where(slot == r, spin(res_ref[r * PH : (r + 1) * PH, :], 2 * r), packed)
    side = [
        merged(
            lat_a_ref[2 * NF + v * PH : 2 * NF + (v + 1) * PH, :],
            lat_b_ref[2 * NF + v * PH : 2 * NF + (v + 1) * PH, :],
        )
        for v in range(NV)
    ]
    for u in range(NV):
        turned = 0.1 * sum(jac_ref[2, u, v] * side[v] for v in range(NV))
        corr = 0.2 * packed * side[u] + jnp.where(even_lane, turned, -turned)
        for r in range(RAD):
            rows = slice((u * RAD + r) * PH, (u * RAD + r + 1) * PH)
            o_ref[rows, :] = part_ref[rows, :] + jnp.where(edge, spin(corr, -2 * r), 0.0)
    for last in range(2):
        near = 0.2 * res_ref[pl.ds(last * (PH - 1), RAD, stride=PH), :]
        rows = []
        for v in range(NV):
            at = KF + v * RAD
            a, b = lon_a_ref[at : at + RAD, :], lon_b_ref[at : at + RAD, :]
            rows.append(jnp.where(odd, b, a) if last else jnp.where(odd, a, b))
        for u in range(NV):
            turned = 0.1 * sum(jac_ref[1, u, v] * rows[v] for v in range(NV))
            where = pl.ds(u * RAD * PH + last * (PH - 1), RAD, stride=PH)
            added = near * rows[u] + (-turned if last else turned)
            o_ref[where, :] = o_ref[where, :] + added


def pick_kernel(got_ref, fp_ref, o_ref, count_ref):
    def visit(p, block, rank):
        o_ref[p : p + 1, :] = got_ref[block, pl.ds(rank, 1), :]

    rank_rows(fp_ref, count_ref, visit)


def call(kernel, name, ins, outs, specs=None, scratch=(), flops=0, moved=0):
    shapes = [jax.ShapeDtypeStruct(s, F32) for s in outs]
    single = len(shapes) == 1
    return pl.pallas_call(
        kernel,
        out_shape=shapes[0] if single else shapes,
        in_specs=specs or [VMEM] * len(ins),
        out_specs=VMEM if single else [VMEM] * len(shapes),
        scratch_shapes=list(scratch),
        compiler_params=PARAMS,
        cost_estimate=pl.CostEstimate(flops=flops, bytes_accessed=moved, transcendentals=0),
        name=name,
    )(*ins)


def swaps(count, first, periodic):
    pairs = []
    for i in range(first, count, 2):
        if i + 1 < count or periodic:
            j = (i + 1) % count
            pairs += [(i, j), (j, i)]
    return pairs


def exchange(lon_a, lon_b, lat):
    ring = ("comp", "lon")
    size = lax.axis_size("comp") * lax.axis_size("lon")
    width = lax.axis_size("lat")
    got_lat = [lax.ppermute(lat, "lat", swaps(width, first, False)) for first in (0, 1)]
    got_lon = [
        lax.ppermute(block, ring, swaps(size, first, True))
        for first, block in enumerate((lon_a, lon_b))
    ]
    return (*got_lon, *got_lat)


def shards(
    shell,
    resistivity,
    jacobians,
    current_weights,
    footpoint,
    footrow,
    slab,
    conductance,
    chemistry,
    coupling,
    potential_weights,
):
    slab_rows = slab.reshape(NF * LEV * LON, TH)
    shell_rows = shell.reshape(SHELL_ROWS * PH, TH)
    s2, lon_a, lon_b, lat = call(
        pack_kernel,
        "pack",
        (slab_rows, shell_rows),
        [(LON, KF, TH), (KF + SHELL_ROWS, TH), (KF + SHELL_ROWS, TH), (2 * NF + NV * PH, TH)],
        moved=8_000_000,
    )
    halos = exchange(lon_a, lon_b, lat)
    part = call(
        shell_kernel,
        "shell",
        (shell, resistivity, jacobians),
        [shell.shape],
        specs=[VMEM, VMEM, SMEM],
        flops=30_000_000,
        moved=5_000_000,
    )
    middle = call(
        step_kernel, "step", (s2, conductance, chemistry), [(LON, KF, TH)], flops=60_000_000, moved=5_000_000
    )
    first = pl.BlockSpec((NV, 1, PH, TH), lambda i: (0, 0, 0, 0))
    send = pl.pallas_call(
        current_kernel,
        grid=(1,),
        out_shape=jax.ShapeDtypeStruct((BLOCKS, 8, TH), F32),
        in_specs=[first, pl.BlockSpec((1, PH, TH), lambda i: (0, 0, 0)), SMEM, SMEM, SMEM, SMEM]
        + [VMEM] * 4,
        out_specs=VMEM,
        scratch_shapes=[pltpu.VMEM((PH, TH), F32), pltpu.SMEM((BLOCKS,), jnp.int32)],
        compiler_params=PARAMS,
        name="current",
    )(part, resistivity, jacobians, current_weights, footpoint, footrow, *halos)
    got = lax.all_to_all(send, "lon", split_axis=0, concat_axis=0, tiled=True)
    middle, source, lon_a, lon_b, lat = call(
        middle_kernel,
        "middle",
        (middle, *halos, conductance, coupling, got),
        [(LON, KF, TH), (LON, TH), (KF, TH), (KF, TH), (2 * NF, TH)],
        moved=6_000_000,
    )
    ends = exchange(lon_a, lon_b, lat)
    shell_next = call(
        shell_edge_kernel,
        "shell_edge",
        (part.reshape(SHELL_ROWS * PH, TH), resistivity.reshape(RAD * PH, TH), jacobians, *halos),
        [(SHELL_ROWS * PH, TH)],
        specs=[VMEM, VMEM, SMEM] + [VMEM] * 4,
        scratch=[pltpu.VMEM((PH, TH), F32)],
        moved=4_000_000,
    ).reshape(shell.shape)
    last = call(
        step_kernel, "step", (middle, conductance, chemistry), [(LON, KF, TH)], flops=60_000_000, moved=5_000_000
    )
    asked = call(
        potential_kernel,
        "potential",
        (last, *ends, conductance, coupling, potential_weights.reshape(1, NF), source, got),
        [(BLOCKS, 8, TH)],
        scratch=[pltpu.VMEM((LON, TH), F32)],
    )
    back = lax.all_to_all(asked, "lon", split_axis=0, concat_axis=0, tiled=True)
    slab_next = call(
        finish_kernel,
        "finish",
        (last, *ends, conductance, coupling, source),
        [(NF * LEV * LON, TH)],
        moved=5_000_000,
    ).reshape(slab.shape)
    boundary = call(
        pick_kernel,
        "pick",
        (back, footpoint),
        [(PH, TH)],
        specs=[VMEM, SMEM],
        scratch=[pltpu.SMEM((BLOCKS,), jnp.int32)],
    )
    return shell_next, slab_next, boundary


def solution(mesh):
    ring = ("comp", "lon")
    placed = (
        P(None, None, ring, "lat"),
        P(None, ring, "lat"),
        P(),
        P(),
        P("lat", ring, None),
        P("lat", ring),
        P(None, None, ring, "lat"),
        P(ring, "lat"),
        P(),
        P(),
        P(),
    )
    return jax.shard_map(
        shards,
        mesh=mesh,
        in_specs=placed,
        out_specs=(P(None, None, ring, "lat"), P(None, None, ring, "lat"), P(ring, "lat")),
        check_vma=False,
    )
```

```python
import functools

import jax
import jax.numpy as jnp
from jax import lax
from jax.experimental import pallas as pl
from jax.experimental.pallas import tpu as pltpu
from jax.sharding import PartitionSpec as P

NV = 8
NF = 40
RAD = 32
PH = 16
TH = 128
LEV = 8
LON = 16
BLOCKS = 16
KF = LEV * NF
SHELL_ROWS = NV * RAD
F32 = jnp.float32
BF16 = jnp.bfloat16
VMEM = pl.BlockSpec(memory_space=pltpu.VMEM)
SMEM = pl.BlockSpec(memory_space=pltpu.SMEM)
HBM = pl.BlockSpec(memory_space=pltpu.HBM)
DMA = pltpu.SemaphoreType.DMA
PARAMS = pltpu.CompilerParams(vmem_limit_bytes=24 * 1024 * 1024)


def go(source, target, sem):
    copy = pltpu.make_async_copy(source, target, sem)
    copy.start()
    return copy


def odd_lon():
    return lax.rem(lax.axis_index("lon"), 2) == 1


def odd_lat():
    return lax.rem(lax.axis_index("lat"), 2) == 1


def lanes(rows):
    return lax.broadcasted_iota(jnp.int32, (rows, TH), 1)


def slot_of(rows):
    return lax.rem(lanes(rows) + 1, TH) // 2


def edge_of(rows):
    lane = lanes(rows)
    return (lane == 0) | (lane == TH - 1)


def spin(x, shift):
    shift = shift % TH
    return x if shift == 0 else pltpu.roll(x, shift, 1)


def merged(first, second):
    odd = odd_lat()
    left = jnp.where(odd, first, second)
    right = jnp.where(odd, second, first)
    even_lane = lax.rem(lanes(left.shape[0]), 2) == 0
    return jnp.where(even_lane, spin(left, 1), spin(right, -1))


def load_level(slab_ref, s2_ref, sems, k):
    for l in range(LON):
        go(slab_ref.at[:, k, l, :], s2_ref.at[l, k * NF : (k + 1) * NF, :], sems.at[k])


def wait_level(s2_ref, sems, k):
    part = s2_ref.at[:, k * NF : (k + 1) * NF, :]
    pltpu.make_async_copy(part, part, sems.at[k]).wait()


def pack_level(s2_ref, k, slot, acc):
    for l in range(LON):
        j = l + LON * (k % 4)
        acc = jnp.where(slot == j, spin(s2_ref[l, k * NF : (k + 1) * NF, :], 2 * j), acc)
    return acc


def pack_kernel(slab_ref, shell_ref, lon_a_ref, lon_b_ref, lat_ref, s2_ref, sh_ref, slab_sems, shell_sems):
    copies = [
        go(
            shell_ref.at[v * RAD * PH : (v + 1) * RAD * PH],
            sh_ref.at[v * RAD * PH : (v + 1) * RAD * PH],
            shell_sems.at[v],
        )
        for v in range(NV)
    ]
    odd = odd_lon()
    slot = slot_of(PH)
    for v in range(NV):
        load_level(slab_ref, s2_ref, slab_sems, v)
        copies[v].wait()
        acc = jnp.zeros((PH, TH), F32)
        for r in range(RAD):
            x = sh_ref[(v * RAD + r) * PH : (v * RAD + r + 1) * PH, :]
            acc = jnp.where(slot == r, spin(x, 2 * r), acc)
        lat_ref[2 * NF + v * PH : 2 * NF + (v + 1) * PH, :] = acc
        low = sh_ref[pl.ds(v * RAD * PH, RAD, stride=PH), :]
        high = sh_ref[pl.ds(v * RAD * PH + PH - 1, RAD, stride=PH), :]
        at = KF + v * RAD
        lon_a_ref[at : at + RAD, :] = jnp.where(odd, low, high)
        lon_b_ref[at : at + RAD, :] = jnp.where(odd, high, low)
    slot = slot_of(NF)
    for half in range(2):
        acc = jnp.zeros((NF, TH), F32)
        for k in range(4 * half, 4 * half + 4):
            wait_level(s2_ref, slab_sems, k)
            acc = pack_level(s2_ref, k, slot, acc)
        lat_ref[half * NF : (half + 1) * NF, :] = acc
    low, high = s2_ref[0], s2_ref[LON - 1]
    lon_a_ref[0:KF, :] = jnp.where(odd, low, high)
    lon_b_ref[0:KF, :] = jnp.where(odd, high, low)


def mixing_matrix(chem):
    rows = (lax.broadcasted_iota(jnp.int32, (2 * NF, NF), 0) % NF) == lax.broadcasted_iota(
        jnp.int32, (2 * NF, NF), 1
    )
    cols = lax.broadcasted_iota(jnp.int32, (NF, 6 * NF), 0) == (
        lax.broadcasted_iota(jnp.int32, (NF, 6 * NF), 1) % NF
    )
    wide = jnp.dot(
        jnp.dot(
            rows.astype(F32), chem, precision=lax.Precision.HIGHEST, preferred_element_type=F32
        ),
        cols.astype(F32),
        precision=lax.Precision.HIGHEST,
        preferred_element_type=F32,
    )
    i = lax.broadcasted_iota(jnp.int32, (2 * NF, 6 * NF), 0)
    j = lax.broadcasted_iota(jnp.int32, (2 * NF, 6 * NF), 1)
    wide = jnp.where((i // NF) == ((j // NF) % 2), 0.1 * wide, 0.0)
    high = wide.astype(BF16).astype(F32)
    return jnp.where(j < 4 * NF, high, wide - high).astype(BF16)


def step(x_ref, cond_ref, chem_ref, o_ref):
    lhs = mixing_matrix(chem_ref[...])
    lane = lanes(2 * NF)
    zero = jnp.zeros((NF, TH), F32)

    def body(g, carry):
        for kp in range(LEV // 2):
            rows = slice(2 * NF * kp, 2 * NF * (kp + 1))
            xs = [x_ref[2 * g, rows, :], x_ref[2 * g + 1, rows, :]]
            below = x_ref[jnp.maximum(2 * g - 1, 0), rows, :] * jnp.where(g > 0, 1.0, 0.0)
            above = x_ref[jnp.minimum(2 * g + 2, LON - 1), rows, :] * jnp.where(
                g < LON // 2 - 1, 1.0, 0.0
            )
            near = [below + xs[1], xs[0] + above]
            both = jnp.concatenate(xs, axis=1)
            high = both.astype(BF16)
            low = (both - high.astype(F32)).astype(BF16)
            mixed = jnp.dot(
                lhs, jnp.concatenate([high, low, high], axis=0), preferred_element_type=F32
            )
            for i in range(2):
                x = xs[i]
                l = 2 * g + i
                if kp == 0:
                    down = jnp.concatenate([zero, x[:NF]], axis=0)
                else:
                    down = x_ref[l, 2 * NF * kp - NF : 2 * NF * kp + NF, :]
                if kp == LEV // 2 - 1:
                    up = jnp.concatenate([x[NF:], zero], axis=0)
                else:
                    up = x_ref[l, 2 * NF * kp + NF : 2 * NF * kp + 3 * NF, :]
                sides = jnp.where(lane == 0, 0.0, spin(x, 1)) + jnp.where(
                    lane == TH - 1, 0.0, spin(x, -1)
                )
                c = 0.1 * cond_ref[pl.ds(l, 1), :]
                o_ref[l, rows, :] = (
                    x * (0.8 - 4.0 * c)
                    + c * (near[i] + sides)
                    + 0.1 * (up + down)
                    + mixed[:, i * TH : (i + 1) * TH]
                )
        return carry

    lax.fori_loop(0, LON // 2, body, 0)


def shell_matrices(jac_ref):
    size = NV * PH
    spread = (
        lax.broadcasted_iota(jnp.int32, (size, NV), 0) // PH
        == lax.broadcasted_iota(jnp.int32, (size, NV), 1)
    ).astype(F32)
    gather = (
        lax.broadcasted_iota(jnp.int32, (NV, size), 0)
        == lax.broadcasted_iota(jnp.int32, (NV, size), 1) // PH
    ).astype(F32)
    i = lax.broadcasted_iota(jnp.int32, (size, size), 0)
    j = lax.broadcasted_iota(jnp.int32, (size, size), 1)
    apart = (j % PH) - (i % PH)

    def wide(d):
        half = jnp.dot(
            spread, jac_ref[d], precision=lax.Precision.HIGHEST, preferred_element_type=F32
        )
        return 0.1 * jnp.dot(
            half, gather, precision=lax.Precision.HIGHEST, preferred_element_type=F32
        )

    turn = wide(1)
    parts = [
        jnp.where(apart == 1, turn, jnp.where(apart == -1, -turn, 0.0)),
        jnp.where(apart == 0, wide(0), 0.0),
        jnp.where(apart == 0, wide(2), 0.0),
    ]
    high = [part.astype(BF16) for part in parts]
    low = [(part - h.astype(F32)).astype(BF16) for part, h in zip(parts, high)]
    same = (i // PH) == (j // PH)
    sums = jnp.where(same & ((apart == 1) | (apart == -1)), 1.0, 0.0).astype(BF16)
    return jnp.concatenate(high + high + low, axis=1), jnp.concatenate([sums, sums], axis=1)


def halves(x):
    high = x.astype(BF16)
    return high, (x - high.astype(F32)).astype(BF16)


def shell_part(x_ref, res_ref, jac_ref, o_ref, done):
    flux_of, sums_of = shell_matrices(jac_ref)
    lane = lanes(NV * PH)

    def rows_of(r):
        return jnp.concatenate([x_ref[v, r] for v in range(NV)], axis=0)

    def body(g, carry):
        r = 2 * g
        below = rows_of(jnp.maximum(r - 1, 0)) * jnp.where(g > 0, 1.0, 0.0)
        x = [rows_of(r), rows_of(r + 1)]
        above = rows_of(jnp.minimum(r + 2, RAD - 1)) * jnp.where(g < RAD // 2 - 1, 1.0, 0.0)
        radial = jnp.concatenate([x[1] - below, above - x[0]], axis=1)
        south = [jnp.where(lane == 0, 0.0, spin(a, 1)) for a in x]
        north = [jnp.where(lane == TH - 1, 0.0, spin(a, -1)) for a in x]
        polar = jnp.concatenate([n - s for n, s in zip(north, south)], axis=1)
        xh, xl = halves(jnp.concatenate(x, axis=1))
        rh, rl = halves(radial)
        ph, pl_ = halves(polar)
        flux = jnp.dot(
            flux_of,
            jnp.concatenate([xh, rh, ph, xl, rl, pl_, xh, rh, ph], axis=0),
            preferred_element_type=F32,
        )
        sums = jnp.dot(
            sums_of, jnp.concatenate([xh, xl], axis=0), preferred_element_type=F32
        )
        around = [below + x[1], x[0] + above]
        for i in range(2):
            at = slice(i * TH, (i + 1) * TH)
            lap = (around[i] + sums[:, at]) + (south[i] + north[i]) - 6.0 * x[i]
            res = 0.2 * res_ref[pl.ds(pl.multiple_of((r + i) * PH, PH), PH), :]
            for v in range(NV):
                rows = slice(v * PH, (v + 1) * PH)
                o_ref[v, r + i] = x[i][rows] + res * lap[rows] - flux[rows, at]
        done(r)
        return carry

    lax.fori_loop(0, RAD // 2, body, 0)


def interior_kernel(
    slab_ref, shell_ref, res_ref, jac_ref, cond_ref, chem_ref,
    m_ref, part_ref, first_ref, near_ref,
    s2_ref, sh_ref, so_ref, rs_ref, slab_sems, sems,
):
    one = go(shell_ref, sh_ref, sems.at[0])
    two = go(res_ref, rs_ref, sems.at[1])
    for k in range(LEV):
        load_level(slab_ref, s2_ref, slab_sems, k)
    two.wait()
    slot = slot_of(PH)
    packed = jnp.zeros((PH, TH), F32)
    for r in range(RAD):
        packed = jnp.where(slot == r, spin(rs_ref[r * PH : (r + 1) * PH, :], 2 * r), packed)
    near_ref[0:PH, :] = rs_ref[0:PH, :]
    near_ref[PH : 2 * PH, :] = packed
    for last in range(2):
        at = 2 * PH + last * RAD
        near_ref[at : at + RAD, :] = rs_ref[pl.ds(last * (PH - 1), RAD, stride=PH), :]
    one.wait()

    def send_shell(r):
        go(so_ref.at[:, pl.ds(r, 2)], part_ref.at[:, pl.ds(r, 2)], sems.at[2])

    shell_part(sh_ref, rs_ref, jac_ref, so_ref, send_shell)
    first_ref[...] = so_ref[:, 0]
    for k in range(LEV):
        wait_level(s2_ref, slab_sems, k)
    step(s2_ref, cond_ref, chem_ref, m_ref)
    pltpu.make_async_copy(so_ref, part_ref, sems.at[2]).wait()


def rank_rows(fp_ref, count_ref, visit):
    for b in range(BLOCKS):
        count_ref[b] = 0
    for p in range(PH):
        block = fp_ref[0, p, 0]
        rank = count_ref[block]
        count_ref[block] = rank + 1
        visit(p, block, rank)


def current_kernel(
    part_ref, res_all_ref, jac_ref, weight_ref, fp_ref, row_ref, lon_a_all, lon_b_all, lat_a_all, lat_b_all,
    send_ref, where_ref, cur_ref, count_ref,
):
    lon_a_ref, lon_b_ref = lon_a_all.at[KF:, :], lon_b_all.at[KF:, :]
    lat_a_ref, lat_b_ref = lat_a_all.at[2 * NF :, :], lat_b_all.at[2 * NF :, :]
    send_ref[...] = jnp.zeros(send_ref.shape, F32)
    w = [weight_ref[v] for v in range(NV)]
    wj = [[sum(w[u] * jac_ref[d, u, v] for u in range(NV)) for v in range(NV)] for d in (1, 2)]
    odd = odd_lon()
    cur = sum(w[v] * part_ref[v] for v in range(NV))
    res = 0.2 * res_all_ref[0:PH, :]
    rows_a = [lon_a_ref[v * RAD : v * RAD + 1, :] for v in range(NV)]
    rows_b = [lon_b_ref[v * RAD : v * RAD + 1, :] for v in range(NV)]
    low = [jnp.where(odd, a, b) for a, b in zip(rows_a, rows_b)]
    high = [jnp.where(odd, b, a) for a, b in zip(rows_a, rows_b)]
    row = lax.broadcasted_iota(jnp.int32, (PH, TH), 0)
    lane = lanes(PH)
    plain = sum(w[v] * low[v] for v in range(NV))
    turned = 0.1 * sum(wj[0][v] * low[v] for v in range(NV))
    cur = cur + jnp.where(row == 0, res * plain + turned, 0.0)
    plain = sum(w[v] * high[v] for v in range(NV))
    turned = 0.1 * sum(wj[0][v] * high[v] for v in range(NV))
    cur = cur + jnp.where(row == PH - 1, res * plain - turned, 0.0)
    side = [
        merged(
            lat_a_ref[v * PH : (v + 1) * PH, :],
            lat_b_ref[v * PH : (v + 1) * PH, :],
        )
        for v in range(NV)
    ]
    plain = sum(w[v] * side[v] for v in range(NV))
    turned = 0.1 * sum(wj[1][v] * side[v] for v in range(NV))
    cur = cur + jnp.where(lane == 0, res * plain + turned, 0.0)
    cur = cur + jnp.where(lane == TH - 1, res * plain - turned, 0.0)
    cur_ref[...] = cur

    def visit(p, block, rank):
        where_ref[p : p + 1, :] = jnp.full((1, TH), 2 * block + rank, jnp.int32).astype(F32)
        send_ref[block, pl.ds(rank, 1), :] = cur_ref[p : p + 1, :]
        send_ref[block, pl.ds(2 + rank, 1), :] = jnp.full((1, TH), row_ref[0, p], jnp.int32).astype(F32)

    rank_rows(fp_ref, count_ref, visit)


def slab_edges(lat_a, lat_b):
    return [
        merged(lat_a[h * NF : (h + 1) * NF, :], lat_b[h * NF : (h + 1) * NF, :]) for h in range(2)
    ]


def column(row):
    diagonal = lax.broadcasted_iota(jnp.int32, (NF, NF), 0) == lax.broadcasted_iota(
        jnp.int32, (NF, NF), 1
    )
    return jnp.broadcast_to(
        jnp.sum(
            jnp.where(diagonal, jnp.broadcast_to(row, (NF, NF)), 0.0), axis=1, keepdims=True
        ),
        (NF, TH),
    )


def put_levels(coupling_ref, level_ref, count):
    for k in range(count):
        level_ref[k * NF : (k + 1) * NF, :] = column(0.1 * coupling_ref[k : k + 1, :])


def gather_source(got_ref):
    row = lax.broadcasted_iota(jnp.int32, (LON, TH), 0).astype(F32)
    source = jnp.zeros((LON, TH), F32)
    for b in range(BLOCKS):
        for s in range(2):
            source = source + jnp.where(
                row == got_ref[b, 2 + s : 3 + s, :], got_ref[b, s : s + 1, :], 0.0
            )
    return source


def fixed_tile(x, l, k, c, edge, side_ref, level_ref, source, end_ref):
    rows = slice(k * NF, (k + 1) * NF)
    j = l + LON * (k % 4)
    h = jnp.where(edge, spin(side_ref[(k // 4) * NF : (k // 4 + 1) * NF, :], -2 * j), 0.0)
    if l == 0:
        h = h + end_ref[0, rows, :]
    if l == LON - 1:
        h = h + end_ref[1, rows, :]
    return x + c * h + level_ref[rows, :] * source


def put_edges(lon_a_ref, lon_b_ref, lat_a_ref, lat_b_ref, side_ref, end_ref):
    odd = odd_lon()
    a, b = lon_a_ref[...], lon_b_ref[...]
    end_ref[0] = jnp.where(odd, a, b)
    end_ref[1] = jnp.where(odd, b, a)
    for at in range(0, side_ref.shape[0], NF):
        side_ref[at : at + NF, :] = merged(lat_a_ref[at : at + NF, :], lat_b_ref[at : at + NF, :])


def middle_kernel(
    x_ref, lon_a_all, lon_b_all, lat_a_all, lat_b_all, cond_ref, coupling_ref, weight_ref, got_ref,
    o_ref, source_ref, next_a_ref, next_b_ref, lat_ref, level_ref,
    side_ref, end_ref,
):
    lon_a_ref, lon_b_ref = lon_a_all.at[0:KF, :], lon_b_all.at[0:KF, :]
    lat_a_ref, lat_b_ref = lat_a_all.at[0 : 2 * NF, :], lat_b_all.at[0 : 2 * NF, :]
    put_levels(coupling_ref, level_ref, LEV)
    level_ref[KF : KF + NF, :] = column(weight_ref[...])
    source_ref[...] = gather_source(got_ref)
    put_edges(lon_a_ref, lon_b_ref, lat_a_ref, lat_b_ref, side_ref, end_ref)
    edge = edge_of(NF)
    slot = slot_of(NF)
    for l in range(LON):
        c = 0.1 * cond_ref[l : l + 1, :]
        source = source_ref[l : l + 1, :]
        for k in range(LEV):
            rows = slice(k * NF, (k + 1) * NF)
            x = fixed_tile(x_ref[l, rows, :], l, k, c, edge, side_ref, level_ref, source, end_ref)
            o_ref[l, rows, :] = x
    for half in range(2):
        acc = jnp.zeros((NF, TH), F32)
        for k in range(4 * half, 4 * half + 4):
            acc = pack_level(o_ref, k, slot, acc)
        lat_ref[half * NF : (half + 1) * NF, :] = acc
    odd = odd_lon()
    low, high = o_ref[0], o_ref[LON - 1]
    next_a_ref[...] = jnp.where(odd, low, high)
    next_b_ref[...] = jnp.where(odd, high, low)


def second_kernel(x_ref, cond_ref, chem_ref, m_ref):
    step(x_ref, cond_ref, chem_ref, m_ref)


def potential_kernel(
    x_ref, lon_a_all, lon_b_all, lat_a_all, lat_b_all, cond_ref, level_ref, source_ref, got_ref,
    send_ref,
    pot_ref, side_ref, end_ref,
):
    lon_a_ref, lon_b_ref = lon_a_all.at[0:NF, :], lon_b_all.at[0:NF, :]
    lat_a_ref, lat_b_ref = lat_a_all.at[0:NF, :], lat_b_all.at[0:NF, :]
    edge = edge_of(NF)
    weight = level_ref[KF : KF + NF, :]
    put_edges(lon_a_ref, lon_b_ref, lat_a_ref, lat_b_ref, side_ref, end_ref)
    for l in range(LON):
        c = 0.1 * cond_ref[l : l + 1, :]
        x = fixed_tile(
            x_ref[l, 0:NF, :], l, 0, c, edge, side_ref, level_ref, source_ref[l : l + 1, :], end_ref
        )
        pot_ref[l : l + 1, :] = jnp.sum(weight * x, axis=0, keepdims=True)
    potential = pot_ref[...]
    row = lax.broadcasted_iota(jnp.int32, (LON, TH), 0).astype(F32)
    for b in range(BLOCKS):
        for s in range(2):
            send_ref[b, s : s + 1, :] = jnp.sum(
                jnp.where(row == got_ref[b, 2 + s : 3 + s, :], potential, 0.0), axis=0, keepdims=True
            )
        send_ref[b, 2:8, :] = jnp.zeros((6, TH), F32)


def finish_kernel(
    x_ref, lon_a_ref, lon_b_ref, lat_a_ref, lat_b_ref, cond_ref, level_ref, source_ref,
    o_ref,
    y_ref, side_ref, end_ref, sem,
):
    edge = edge_of(NF)
    put_edges(lon_a_ref, lon_b_ref, lat_a_ref, lat_b_ref, side_ref, end_ref)
    for l in range(LON):
        c = 0.1 * cond_ref[l : l + 1, :]
        source = source_ref[l : l + 1, :]
        for k in range(LEV):
            rows = slice(k * NF, (k + 1) * NF)
            y_ref[l, rows, :] = fixed_tile(
                x_ref[l, rows, :], l, k, c, edge, side_ref, level_ref, source, end_ref
            )
            go(y_ref.at[l, rows, :], o_ref.at[:, k, l, :], sem)
    pltpu.make_async_copy(y_ref, y_ref, sem).wait()


def shell_edge_kernel(
    part_ref, near_ref, jac_ref, lon_a_all, lon_b_all, lat_a_all, lat_b_all,
    o_ref,
    x_ref, y_ref, corr_ref, add_ref, part_sems, sem,
):
    size = RAD * PH
    loads = [
        go(part_ref.at[v * size : (v + 1) * size], x_ref.at[v * size : (v + 1) * size], part_sems.at[v])
        for v in range(NV)
    ]
    lon_a_ref, lon_b_ref = lon_a_all.at[KF:, :], lon_b_all.at[KF:, :]
    lat_a_ref, lat_b_ref = lat_a_all.at[2 * NF :, :], lat_b_all.at[2 * NF :, :]
    odd = odd_lon()
    edge = edge_of(PH)
    even_lane = lax.rem(lanes(PH), 2) == 0
    packed = 0.2 * near_ref[PH : 2 * PH, :]
    side = [
        merged(lat_a_ref[v * PH : (v + 1) * PH, :], lat_b_ref[v * PH : (v + 1) * PH, :])
        for v in range(NV)
    ]
    for u in range(NV):
        turned = 0.1 * sum(jac_ref[2, u, v] * side[v] for v in range(NV))
        corr_ref[u] = packed * side[u] + jnp.where(even_lane, turned, -turned)
    for last in range(2):
        at = 2 * PH + last * RAD
        near = 0.2 * near_ref[at : at + RAD, :]
        ends = []
        for v in range(NV):
            a, b = lon_a_ref[v * RAD : (v + 1) * RAD, :], lon_b_ref[v * RAD : (v + 1) * RAD, :]
            ends.append(jnp.where(odd, b, a) if last else jnp.where(odd, a, b))
        for u in range(NV):
            turned = 0.1 * sum(jac_ref[1, u, v] * ends[v] for v in range(NV))
            add_ref[last, u] = near * ends[u] + (-turned if last else turned)
    for u in range(NV):
        loads[u].wait()
        corr = corr_ref[u]
        for r in range(RAD):
            rows = slice((u * RAD + r) * PH, (u * RAD + r + 1) * PH)
            y_ref[rows, :] = x_ref[rows, :] + jnp.where(edge, spin(corr, -2 * r), 0.0)
        for last in range(2):
            where = pl.ds(u * size + last * (PH - 1), RAD, stride=PH)
            y_ref[where, :] = y_ref[where, :] + add_ref[last, u]
        go(y_ref.at[u * size : (u + 1) * size], o_ref.at[u * size : (u + 1) * size], sem)
    pltpu.make_async_copy(y_ref, y_ref, sem).wait()


def pick_kernel(got_ref, where_ref, o_ref):
    where = where_ref[...]
    picked = jnp.zeros((PH, TH), F32)
    for b in range(BLOCKS):
        for s in range(2):
            picked = picked + jnp.where(where == float(2 * b + s), got_ref[b, s : s + 1, :], 0.0)
    o_ref[...] = picked


def call(kernel, name, ins, outs, specs, kept=(), scratch=(), flops=0, moved=0):
    ins = [
        pltpu.with_memory_space_constraint(x, pltpu.HBM) if spec is HBM else x
        for x, spec in zip(ins, specs)
    ]
    shapes = [
        pltpu.HBM(shape, F32) if i in kept else jax.ShapeDtypeStruct(shape, F32)
        for i, shape in enumerate(outs)
    ]
    places = [HBM if i in kept else VMEM for i in range(len(outs))]
    single = len(shapes) == 1
    return pl.pallas_call(
        kernel,
        out_shape=shapes[0] if single else shapes,
        in_specs=specs,
        out_specs=places[0] if single else places,
        scratch_shapes=list(scratch),
        compiler_params=PARAMS,
        cost_estimate=pl.CostEstimate(flops=flops, bytes_accessed=moved, transcendentals=0),
        name=name,
    )(*ins)


def swaps(count, first, periodic):
    pairs = []
    for i in range(first, count, 2):
        if i + 1 < count or periodic:
            j = (i + 1) % count
            pairs += [(i, j), (j, i)]
    return pairs


def exchange(lon_a, lon_b, lat):
    ring = ("comp", "lon")
    size = lax.axis_size("comp") * lax.axis_size("lon")
    width = lax.axis_size("lat")
    got_lat = [lax.ppermute(lat, "lat", swaps(width, first, False)) for first in (0, 1)]
    got_lon = [
        lax.ppermute(block, ring, swaps(size, first, True))
        for first, block in enumerate((lon_a, lon_b))
    ]
    return (*got_lon, *got_lat)


def shards(
    shell,
    resistivity,
    jacobians,
    current_weights,
    footpoint,
    footrow,
    slab,
    conductance,
    chemistry,
    coupling,
    potential_weights,
):
    coupling = coupling.T
    slab_scratch = pltpu.VMEM((LON, KF, TH), F32)
    shell_scratch = pltpu.VMEM(shell.shape, F32)
    flat_scratch = pltpu.VMEM((SHELL_ROWS * PH, TH), F32)

    def rows(count):
        return pltpu.VMEM((count, TH), F32)

    lon_a, lon_b, lat = call(
        pack_kernel,
        "pack",
        (slab, shell.reshape(SHELL_ROWS * PH, TH)),
        [(KF + SHELL_ROWS, TH), (KF + SHELL_ROWS, TH), (2 * NF + NV * PH, TH)],
        [HBM, HBM],
        scratch=[slab_scratch, flat_scratch, DMA((LEV,)), DMA((NV,))],
        moved=8_000_000,
    )
    halos = exchange(lon_a, lon_b, lat)
    middle, part, first, near = call(
        interior_kernel,
        "interior",
        (slab, shell, resistivity.reshape(RAD * PH, TH), jacobians, conductance, chemistry),
        [(LON, KF, TH), shell.shape, (NV, PH, TH), (2 * PH + 2 * RAD, TH)],
        [HBM, HBM, HBM, VMEM, VMEM, VMEM],
        kept=(1,),
        scratch=[
            slab_scratch,
            shell_scratch,
            shell_scratch,
            rows(RAD * PH),
            DMA((LEV,)),
            DMA((3,)),
        ],
        flops=90_000_000,
        moved=20_000_000,
    )
    send, where = call(
        current_kernel,
        "current",
        (first, near, jacobians, current_weights, footpoint, footrow, *halos),
        [(BLOCKS, 8, TH), (PH, TH)],
        [VMEM, VMEM, SMEM, SMEM, SMEM, SMEM] + [VMEM] * 4,
        scratch=[rows(PH), pltpu.SMEM((BLOCKS,), jnp.int32)],
    )
    got = lax.all_to_all(send, "lon", split_axis=0, concat_axis=0, tiled=True)
    shell_next = call(
        shell_edge_kernel,
        "shell_edge",
        (part.reshape(SHELL_ROWS * PH, TH), near, jacobians, *halos),
        [(SHELL_ROWS * PH, TH)],
        [HBM, VMEM, SMEM] + [VMEM] * 4,
        kept=(0,),
        scratch=[
            flat_scratch,
            flat_scratch,
            pltpu.VMEM((NV, PH, TH), F32),
            pltpu.VMEM((2, NV, RAD, TH), F32),
            DMA((NV,)),
            DMA,
        ],
        flops=10_000_000,
        moved=8_000_000,
    ).reshape(shell.shape)
    got, shell_next = lax.optimization_barrier((got, shell_next))
    edges = [rows(2 * NF), pltpu.VMEM((2, KF, TH), F32)]
    middle, source, lon_a, lon_b, lat, levels = call(
        middle_kernel,
        "middle",
        (middle, *halos, conductance, coupling, potential_weights.reshape(1, NF), got),
        [(LON, KF, TH), (LON, TH), (KF, TH), (KF, TH), (2 * NF, TH), (KF + NF, TH)],
        [VMEM] * 9,
        scratch=edges,
        moved=8_000_000,
    )
    ends = exchange(lon_a, lon_b, lat)
    last = call(
        second_kernel,
        "second",
        (middle, conductance, chemistry),
        [(LON, KF, TH)],
        [VMEM] * 3,
        flops=60_000_000,
        moved=10_000_000,
    )
    asked = call(
        potential_kernel,
        "potential",
        (last, *ends, conductance, levels, source, got),
        [(BLOCKS, 8, TH)],
        [VMEM] * 9,
        scratch=[rows(LON), rows(NF), pltpu.VMEM((2, NF, TH), F32)],
    )
    back = lax.all_to_all(asked, "lon", split_axis=0, concat_axis=0, tiled=True)
    slab_next = call(
        finish_kernel,
        "finish",
        (last, *ends, conductance, levels, source),
        [slab.shape],
        [VMEM] * 8,
        kept=(0,),
        scratch=[slab_scratch, *edges, DMA],
        moved=8_000_000,
    )
    boundary = call(pick_kernel, "pick", (back, where), [(PH, TH)], [VMEM] * 2)
    return shell_next, slab_next, boundary


def solution(mesh):
    ring = ("comp", "lon")
    placed = (
        P(None, None, ring, "lat"),
        P(None, ring, "lat"),
        P(),
        P(),
        P("lat", ring, None),
        P("lat", ring),
        P(None, None, ring, "lat"),
        P(ring, "lat"),
        P(),
        P(),
        P(),
    )
    return jax.shard_map(
        shards,
        mesh=mesh,
        in_specs=placed,
        out_specs=(P(None, None, ring, "lat"), P(None, None, ring, "lat"), P(ring, "lat")),
        check_vma=False,
    )
```

```python
import functools

import jax
import jax.numpy as jnp
from jax import lax
from jax.experimental import pallas as pl
from jax.experimental.pallas import tpu as pltpu
from jax.sharding import PartitionSpec as P

NV = 8
NF = 40
RAD = 32
PH = 16
TH = 128
LEV = 8
LON = 16
BLOCKS = 16
KF = LEV * NF
SHELL_ROWS = NV * RAD
F32 = jnp.float32
BF16 = jnp.bfloat16
VMEM = pl.BlockSpec(memory_space=pltpu.VMEM)
SMEM = pl.BlockSpec(memory_space=pltpu.SMEM)
HBM = pl.BlockSpec(memory_space=pltpu.HBM)
DMA = pltpu.SemaphoreType.DMA
PARAMS = pltpu.CompilerParams(vmem_limit_bytes=24 * 1024 * 1024)


def go(source, target, sem):
    copy = pltpu.make_async_copy(source, target, sem)
    copy.start()
    return copy


def odd_lon():
    return lax.rem(lax.axis_index("lon"), 2) == 1


def odd_lat():
    return lax.rem(lax.axis_index("lat"), 2) == 1


def lanes(rows):
    return lax.broadcasted_iota(jnp.int32, (rows, TH), 1)


def slot_of(rows):
    return lax.rem(lanes(rows) + 1, TH) // 2


def edge_of(rows):
    lane = lanes(rows)
    return (lane == 0) | (lane == TH - 1)


def spin(x, shift):
    shift = shift % TH
    return x if shift == 0 else pltpu.roll(x, shift, 1)


def merged(first, second):
    odd = odd_lat()
    left = jnp.where(odd, first, second)
    right = jnp.where(odd, second, first)
    even_lane = lax.rem(lanes(left.shape[0]), 2) == 0
    return jnp.where(even_lane, spin(left, 1), spin(right, -1))


def load_level(slab_ref, s2_ref, sem, k):
    for l in range(LON):
        go(slab_ref.at[:, k, l, :], s2_ref.at[l, k * NF : (k + 1) * NF, :], sem)


def level_rows(ref, k):
    return ref.at[:, k * NF : (k + 1) * NF, :]


def wait_level(s2_ref, sems, k):
    part = level_rows(s2_ref, k)
    pltpu.make_async_copy(part, part, sems.at[k]).wait()


def pack_level(s2_ref, k, slot, acc):
    for l in range(LON):
        j = l + LON * (k % 4)
        acc = jnp.where(slot == j, spin(s2_ref[l, k * NF : (k + 1) * NF, :], 2 * j), acc)
    return acc


def pack_kernel(
    slab_ref, shell_ref, lon_a_ref, lon_b_ref, lat_ref,
    s2_ref, sh_ref, slab_sems, shell_sems,
):
    copies = [
        go(
            shell_ref.at[v * RAD * PH : (v + 1) * RAD * PH],
            sh_ref.at[v * RAD * PH : (v + 1) * RAD * PH],
            shell_sems.at[v],
        )
        for v in range(NV)
    ]
    odd = odd_lon()
    slot = slot_of(PH)
    for v in range(NV):
        load_level(slab_ref, s2_ref, slab_sems.at[v], v)
        copies[v].wait()
        acc = jnp.zeros((PH, TH), F32)
        for r in range(RAD):
            x = sh_ref[(v * RAD + r) * PH : (v * RAD + r + 1) * PH, :]
            acc = jnp.where(slot == r, spin(x, 2 * r), acc)
        lat_ref[2 * NF + v * PH : 2 * NF + (v + 1) * PH, :] = acc
        low = sh_ref[pl.ds(v * RAD * PH, RAD, stride=PH), :]
        high = sh_ref[pl.ds(v * RAD * PH + PH - 1, RAD, stride=PH), :]
        at = KF + v * RAD
        lon_a_ref[at : at + RAD, :] = jnp.where(odd, low, high)
        lon_b_ref[at : at + RAD, :] = jnp.where(odd, high, low)
    slot = slot_of(NF)
    for half in range(2):
        acc = jnp.zeros((NF, TH), F32)
        for k in range(4 * half, 4 * half + 4):
            wait_level(s2_ref, slab_sems, k)
            acc = pack_level(s2_ref, k, slot, acc)
        lat_ref[half * NF : (half + 1) * NF, :] = acc
    low, high = s2_ref[0], s2_ref[LON - 1]
    lon_a_ref[0:KF, :] = jnp.where(odd, low, high)
    lon_b_ref[0:KF, :] = jnp.where(odd, high, low)


def mixing_matrix(chem):
    rows = (lax.broadcasted_iota(jnp.int32, (2 * NF, NF), 0) % NF) == lax.broadcasted_iota(
        jnp.int32, (2 * NF, NF), 1
    )
    cols = lax.broadcasted_iota(jnp.int32, (NF, 6 * NF), 0) == (
        lax.broadcasted_iota(jnp.int32, (NF, 6 * NF), 1) % NF
    )
    wide = jnp.dot(
        jnp.dot(
            rows.astype(F32), chem, precision=lax.Precision.HIGHEST, preferred_element_type=F32
        ),
        cols.astype(F32),
        precision=lax.Precision.HIGHEST,
        preferred_element_type=F32,
    )
    i = lax.broadcasted_iota(jnp.int32, (2 * NF, 6 * NF), 0)
    j = lax.broadcasted_iota(jnp.int32, (2 * NF, 6 * NF), 1)
    wide = jnp.where((i // NF) == ((j // NF) % 2), 0.1 * wide, 0.0)
    high = wide.astype(BF16).astype(F32)
    return jnp.where(j < 4 * NF, high, wide - high).astype(BF16)


def step(x_ref, cond_ref, chem_ref, o_ref):
    lhs = mixing_matrix(chem_ref[...])
    lane = lanes(2 * NF)
    zero = jnp.zeros((NF, TH), F32)

    def body(g, carry):
        for kp in range(LEV // 2):
            rows = slice(2 * NF * kp, 2 * NF * (kp + 1))
            xs = [x_ref[2 * g, rows, :], x_ref[2 * g + 1, rows, :]]
            below = x_ref[jnp.maximum(2 * g - 1, 0), rows, :] * jnp.where(g > 0, 1.0, 0.0)
            above = x_ref[jnp.minimum(2 * g + 2, LON - 1), rows, :] * jnp.where(
                g < LON // 2 - 1, 1.0, 0.0
            )
            near = [below + xs[1], xs[0] + above]
            both = jnp.concatenate(xs, axis=1)
            high = both.astype(BF16)
            low = (both - high.astype(F32)).astype(BF16)
            mixed = jnp.dot(
                lhs, jnp.concatenate([high, low, high], axis=0), preferred_element_type=F32
            )
            for i in range(2):
                x = xs[i]
                l = 2 * g + i
                if kp == 0:
                    down = jnp.concatenate([zero, x[:NF]], axis=0)
                else:
                    down = x_ref[l, 2 * NF * kp - NF : 2 * NF * kp + NF, :]
                if kp == LEV // 2 - 1:
                    up = jnp.concatenate([x[NF:], zero], axis=0)
                else:
                    up = x_ref[l, 2 * NF * kp + NF : 2 * NF * kp + 3 * NF, :]
                sides = jnp.where(lane == 0, 0.0, spin(x, 1)) + jnp.where(
                    lane == TH - 1, 0.0, spin(x, -1)
                )
                c = 0.1 * cond_ref[pl.ds(l, 1), :]
                o_ref[l, rows, :] = (
                    x * (0.8 - 4.0 * c)
                    + c * (near[i] + sides)
                    + 0.1 * (up + down)
                    + mixed[:, i * TH : (i + 1) * TH]
                )
        return carry

    lax.fori_loop(0, LON // 2, body, 0, unroll=4)


def shell_matrices(jac_ref):
    size = NV * PH
    spread = (
        lax.broadcasted_iota(jnp.int32, (size, NV), 0) // PH
        == lax.broadcasted_iota(jnp.int32, (size, NV), 1)
    ).astype(F32)
    columns = lax.broadcasted_iota(jnp.int32, (3 * NV, 3 * size), 1)
    gather = (lax.broadcasted_iota(jnp.int32, (3 * NV, 3 * size), 0) == columns // PH).astype(F32)
    i = lax.broadcasted_iota(jnp.int32, (size, size), 0)
    j = lax.broadcasted_iota(jnp.int32, (size, size), 1)
    apart = (j % PH) - (i % PH)
    exact = dict(precision=lax.Precision.HIGHEST, preferred_element_type=F32)
    three = jnp.concatenate([jac_ref[d] for d in range(3)], axis=1)
    spread_out = 0.1 * jnp.dot(jnp.dot(spread, three, **exact), gather, **exact)

    def wide(d):
        return spread_out[:, d * size : (d + 1) * size]

    turn = wide(1)
    parts = [
        jnp.where(apart == 1, turn, jnp.where(apart == -1, -turn, 0.0)),
        jnp.where(apart == 0, wide(0), 0.0),
        jnp.where(apart == 0, wide(2), 0.0),
    ]
    high = [part.astype(BF16) for part in parts]
    low = [(part - h.astype(F32)).astype(BF16) for part, h in zip(parts, high)]
    same = (i // PH) == (j // PH)
    sums = jnp.where(same & ((apart == 1) | (apart == -1)), 1.0, 0.0).astype(BF16)
    return jnp.concatenate(high + high + low, axis=1), jnp.concatenate([sums, sums], axis=1)


def halves(x):
    high = x.astype(BF16)
    return high, (x - high.astype(F32)).astype(BF16)


def shell_part(x_ref, res_ref, jac_ref, o_ref, done):
    flux_of, sums_of = shell_matrices(jac_ref)
    lane = lanes(NV * PH)

    def rows_of(r):
        return jnp.concatenate([x_ref[v, r] for v in range(NV)], axis=0)

    def body(g, carry):
        r = 2 * g
        below = rows_of(jnp.maximum(r - 1, 0)) * jnp.where(g > 0, 1.0, 0.0)
        x = [rows_of(r), rows_of(r + 1)]
        above = rows_of(jnp.minimum(r + 2, RAD - 1)) * jnp.where(g < RAD // 2 - 1, 1.0, 0.0)
        radial = jnp.concatenate([x[1] - below, above - x[0]], axis=1)
        south = [jnp.where(lane == 0, 0.0, spin(a, 1)) for a in x]
        north = [jnp.where(lane == TH - 1, 0.0, spin(a, -1)) for a in x]
        polar = jnp.concatenate([n - s for n, s in zip(north, south)], axis=1)
        xh, xl = halves(jnp.concatenate(x, axis=1))
        rh, rl = halves(radial)
        ph, pl_ = halves(polar)
        flux = jnp.dot(
            flux_of,
            jnp.concatenate([xh, rh, ph, xl, rl, pl_, xh, rh, ph], axis=0),
            preferred_element_type=F32,
        )
        sums = jnp.dot(
            sums_of, jnp.concatenate([xh, xl], axis=0), preferred_element_type=F32
        )
        around = [below + x[1], x[0] + above]
        for i in range(2):
            at = slice(i * TH, (i + 1) * TH)
            lap = (around[i] + sums[:, at]) + (south[i] + north[i]) - 6.0 * x[i]
            res = 0.2 * res_ref[pl.ds(pl.multiple_of((r + i) * PH, PH), PH), :]
            for v in range(NV):
                rows = slice(v * PH, (v + 1) * PH)
                o_ref[v, r + i] = x[i][rows] + res * lap[rows] - flux[rows, at]
        done(r)
        return carry

    lax.fori_loop(0, RAD // 2, body, 0, unroll=4)


def interior_kernel(
    slab_ref, shell_ref, res_ref, jac_ref, cond_ref, chem_ref,
    m_ref, part_ref, first_ref, near_ref,
    s2_ref, sh_ref, so_ref, rs_ref, sems,
):
    one = go(shell_ref, sh_ref, sems.at[0])
    two = go(res_ref, rs_ref, sems.at[1])
    for k in range(LEV):
        load_level(slab_ref, s2_ref, sems.at[3], k)
    two.wait()
    slot = slot_of(PH)
    packed = jnp.zeros((PH, TH), F32)
    for r in range(RAD):
        packed = jnp.where(slot == r, spin(rs_ref[r * PH : (r + 1) * PH, :], 2 * r), packed)
    near_ref[0:PH, :] = rs_ref[0:PH, :]
    near_ref[PH : 2 * PH, :] = packed
    for last in range(2):
        at = 2 * PH + last * RAD
        near_ref[at : at + RAD, :] = rs_ref[pl.ds(last * (PH - 1), RAD, stride=PH), :]
    one.wait()

    def send_shell(r):
        go(so_ref.at[:, pl.ds(r, 2)], part_ref.at[:, pl.ds(r, 2)], sems.at[2])

    shell_part(sh_ref, rs_ref, jac_ref, so_ref, send_shell)
    first_ref[...] = so_ref[:, 0]
    pltpu.make_async_copy(s2_ref, s2_ref, sems.at[3]).wait()
    step(s2_ref, cond_ref, chem_ref, m_ref)
    pltpu.make_async_copy(so_ref, part_ref, sems.at[2]).wait()


def rank_rows(fp_ref, count_ref, visit):
    for b in range(BLOCKS):
        count_ref[b] = 0
    for p in range(PH):
        block = fp_ref[0, p, 0]
        rank = count_ref[block]
        count_ref[block] = rank + 1
        visit(p, block, rank)


def current_kernel(
    part_ref, res_all_ref, jac_ref, weight_ref, fp_ref, row_ref, lon_a_all, lon_b_all, lat_a_all, lat_b_all,
    send_ref, where_ref, cur_ref, count_ref,
):
    lon_a_ref, lon_b_ref = lon_a_all.at[KF:, :], lon_b_all.at[KF:, :]
    lat_a_ref, lat_b_ref = lat_a_all.at[2 * NF :, :], lat_b_all.at[2 * NF :, :]
    send_ref[...] = jnp.zeros(send_ref.shape, F32)
    w = [weight_ref[v] for v in range(NV)]
    wj = [[sum(w[u] * jac_ref[d, u, v] for u in range(NV)) for v in range(NV)] for d in (1, 2)]
    odd = odd_lon()
    cur = sum(w[v] * part_ref[v] for v in range(NV))
    res = 0.2 * res_all_ref[0:PH, :]
    rows_a = [lon_a_ref[v * RAD : v * RAD + 1, :] for v in range(NV)]
    rows_b = [lon_b_ref[v * RAD : v * RAD + 1, :] for v in range(NV)]
    low = [jnp.where(odd, a, b) for a, b in zip(rows_a, rows_b)]
    high = [jnp.where(odd, b, a) for a, b in zip(rows_a, rows_b)]
    row = lax.broadcasted_iota(jnp.int32, (PH, TH), 0)
    lane = lanes(PH)
    plain = sum(w[v] * low[v] for v in range(NV))
    turned = 0.1 * sum(wj[0][v] * low[v] for v in range(NV))
    cur = cur + jnp.where(row == 0, res * plain + turned, 0.0)
    plain = sum(w[v] * high[v] for v in range(NV))
    turned = 0.1 * sum(wj[0][v] * high[v] for v in range(NV))
    cur = cur + jnp.where(row == PH - 1, res * plain - turned, 0.0)
    side = [
        merged(
            lat_a_ref[v * PH : (v + 1) * PH, :],
            lat_b_ref[v * PH : (v + 1) * PH, :],
        )
        for v in range(NV)
    ]
    plain = sum(w[v] * side[v] for v in range(NV))
    turned = 0.1 * sum(wj[1][v] * side[v] for v in range(NV))
    cur = cur + jnp.where(lane == 0, res * plain + turned, 0.0)
    cur = cur + jnp.where(lane == TH - 1, res * plain - turned, 0.0)
    cur_ref[...] = cur

    def visit(p, block, rank):
        where_ref[p : p + 1, :] = jnp.full((1, TH), 2 * block + rank, jnp.int32).astype(F32)
        send_ref[block, pl.ds(rank, 1), :] = cur_ref[p : p + 1, :]
        send_ref[block, pl.ds(2 + rank, 1), :] = jnp.full((1, TH), row_ref[0, p], jnp.int32).astype(F32)

    rank_rows(fp_ref, count_ref, visit)


def slab_edges(lat_a, lat_b):
    return [
        merged(lat_a[h * NF : (h + 1) * NF, :], lat_b[h * NF : (h + 1) * NF, :]) for h in range(2)
    ]


def column(row):
    diagonal = lax.broadcasted_iota(jnp.int32, (NF, NF), 0) == lax.broadcasted_iota(
        jnp.int32, (NF, NF), 1
    )
    return jnp.broadcast_to(
        jnp.sum(
            jnp.where(diagonal, jnp.broadcast_to(row, (NF, NF)), 0.0), axis=1, keepdims=True
        ),
        (NF, TH),
    )


def put_levels(coupling_ref, level_ref, count):
    for k in range(count):
        level_ref[k * NF : (k + 1) * NF, :] = column(0.1 * coupling_ref[k : k + 1, :])


def gather_source(got_ref):
    row = lax.broadcasted_iota(jnp.int32, (LON, TH), 0).astype(F32)
    source = jnp.zeros((LON, TH), F32)
    for b in range(BLOCKS):
        for s in range(2):
            source = source + jnp.where(
                row == got_ref[b, 2 + s : 3 + s, :], got_ref[b, s : s + 1, :], 0.0
            )
    return source


def fixed_tile(x, l, k, c, edge, side_ref, level_ref, source, end_ref):
    rows = slice(k * NF, (k + 1) * NF)
    j = l + LON * (k % 4)
    h = jnp.where(edge, spin(side_ref[(k // 4) * NF : (k // 4 + 1) * NF, :], -2 * j), 0.0)
    if l == 0:
        h = h + end_ref[0, rows, :]
    if l == LON - 1:
        h = h + end_ref[1, rows, :]
    return x + c * h + level_ref[rows, :] * source


def put_edges(lon_a_ref, lon_b_ref, lat_a_ref, lat_b_ref, side_ref, end_ref):
    odd = odd_lon()
    a, b = lon_a_ref[...], lon_b_ref[...]
    end_ref[0] = jnp.where(odd, a, b)
    end_ref[1] = jnp.where(odd, b, a)
    for at in range(0, side_ref.shape[0], NF):
        side_ref[at : at + NF, :] = merged(lat_a_ref[at : at + NF, :], lat_b_ref[at : at + NF, :])


def middle_kernel(
    x_ref, lon_a_all, lon_b_all, lat_a_all, lat_b_all, cond_ref, level_all, got_ref,
    o_ref, source_ref, next_a_ref, next_b_ref, lat_ref,
    level_ref, side_ref, end_ref, sem,
):
    copy = go(level_all, level_ref, sem)
    lon_a_ref, lon_b_ref = lon_a_all.at[0:KF, :], lon_b_all.at[0:KF, :]
    lat_a_ref, lat_b_ref = lat_a_all.at[0 : 2 * NF, :], lat_b_all.at[0 : 2 * NF, :]
    source_ref[...] = gather_source(got_ref)
    put_edges(lon_a_ref, lon_b_ref, lat_a_ref, lat_b_ref, side_ref, end_ref)
    edge = edge_of(NF)
    slot = slot_of(NF)
    copy.wait()
    for l in range(LON):
        c = 0.1 * cond_ref[l : l + 1, :]
        source = source_ref[l : l + 1, :]
        for k in range(LEV):
            rows = slice(k * NF, (k + 1) * NF)
            x = fixed_tile(x_ref[l, rows, :], l, k, c, edge, side_ref, level_ref, source, end_ref)
            o_ref[l, rows, :] = x
    for half in range(2):
        acc = jnp.zeros((NF, TH), F32)
        for k in range(4 * half, 4 * half + 4):
            acc = pack_level(o_ref, k, slot, acc)
        lat_ref[half * NF : (half + 1) * NF, :] = acc
    odd = odd_lon()
    low, high = o_ref[0], o_ref[LON - 1]
    next_a_ref[...] = jnp.where(odd, low, high)
    next_b_ref[...] = jnp.where(odd, high, low)


def second_kernel(
    x_ref, cond_ref, chem_ref, coupling_ref, weight_ref, m_ref, level_ref, near_ref, last_ref, sems
):
    copies = [go(coupling_ref, near_ref, sems.at[0]), go(weight_ref, last_ref, sems.at[1])]
    step(x_ref, cond_ref, chem_ref, m_ref)
    for copy in copies:
        copy.wait()
    put_levels(near_ref, level_ref, LEV)
    level_ref[KF : KF + NF, :] = column(last_ref[...])


def potential_kernel(
    x_ref, lon_a_all, lon_b_all, lat_a_all, lat_b_all, cond_ref, level_ref, source_ref, got_ref,
    send_ref,
    pot_ref, side_ref, end_ref,
):
    lon_a_ref, lon_b_ref = lon_a_all.at[0:NF, :], lon_b_all.at[0:NF, :]
    lat_a_ref, lat_b_ref = lat_a_all.at[0:NF, :], lat_b_all.at[0:NF, :]
    edge = edge_of(NF)
    weight = level_ref[KF : KF + NF, :]
    put_edges(lon_a_ref, lon_b_ref, lat_a_ref, lat_b_ref, side_ref, end_ref)
    for l in range(LON):
        c = 0.1 * cond_ref[l : l + 1, :]
        x = fixed_tile(
            x_ref[l, 0:NF, :], l, 0, c, edge, side_ref, level_ref, source_ref[l : l + 1, :], end_ref
        )
        pot_ref[l : l + 1, :] = jnp.sum(weight * x, axis=0, keepdims=True)
    potential = pot_ref[...]
    row = lax.broadcasted_iota(jnp.int32, (LON, TH), 0).astype(F32)
    for b in range(BLOCKS):
        for s in range(2):
            send_ref[b, s : s + 1, :] = jnp.sum(
                jnp.where(row == got_ref[b, 2 + s : 3 + s, :], potential, 0.0), axis=0, keepdims=True
            )
        send_ref[b, 2:8, :] = jnp.zeros((6, TH), F32)


def finish_kernel(
    x_ref, lon_a_ref, lon_b_ref, lat_a_ref, lat_b_ref, cond_ref, level_ref, source_ref,
    o_ref,
    y_ref, side_ref, end_ref, sem,
):
    edge = edge_of(NF)
    put_edges(lon_a_ref, lon_b_ref, lat_a_ref, lat_b_ref, side_ref, end_ref)
    for l in range(LON):
        c = 0.1 * cond_ref[l : l + 1, :]
        source = source_ref[l : l + 1, :]
        for k in range(LEV):
            rows = slice(k * NF, (k + 1) * NF)
            y_ref[l, rows, :] = fixed_tile(
                x_ref[l, rows, :], l, k, c, edge, side_ref, level_ref, source, end_ref
            )
            go(y_ref.at[l, rows, :], o_ref.at[:, k, l, :], sem)
    pltpu.make_async_copy(y_ref, y_ref, sem).wait()


def shell_edge_tile(u, x_ref, y_ref, o_ref, corr, adds, edge, sem):
    size = RAD * PH
    for r in range(RAD):
        rows = slice((u * RAD + r) * PH, (u * RAD + r + 1) * PH)
        y_ref[rows, :] = x_ref[rows, :] + jnp.where(edge, spin(corr, -2 * r), 0.0)
    for last in range(2):
        where = pl.ds(u * size + last * (PH - 1), RAD, stride=PH)
        y_ref[where, :] = y_ref[where, :] + adds[last]
    go(y_ref.at[u * size : (u + 1) * size], o_ref.at[u * size : (u + 1) * size], sem)


def load_part(part_ref, x_ref, part_sems, these):
    size = RAD * PH
    return {
        u: go(
            part_ref.at[u * size : (u + 1) * size], x_ref.at[u * size : (u + 1) * size], part_sems.at[u]
        )
        for u in these
    }


def wait_half(y_ref, first, sem):
    half = NV // 2 * RAD * PH
    part = y_ref.at[first * half : (first + 1) * half]
    pltpu.make_async_copy(part, part, sem).wait()


def shell_edge_kernel(
    part_ref, near_ref, jac_ref, lon_a_all, lon_b_all, lat_a_all, lat_b_all, coupling_ref,
    o_ref, keep_ref, level_all,
    x_ref, y_ref, add_ref, cols_ref, level_ref, part_sems, sems,
):
    copy = go(coupling_ref, cols_ref, sems.at[2])
    loads = load_part(part_ref, x_ref, part_sems, range(NV // 2))
    lon_a_ref, lon_b_ref = lon_a_all.at[KF:, :], lon_b_all.at[KF:, :]
    lat_a_ref, lat_b_ref = lat_a_all.at[2 * NF :, :], lat_b_all.at[2 * NF :, :]
    odd = odd_lon()
    edge = edge_of(PH)
    even_lane = lax.rem(lanes(PH), 2) == 0
    packed = 0.2 * near_ref[PH : 2 * PH, :]
    side = [
        merged(lat_a_ref[v * PH : (v + 1) * PH, :], lat_b_ref[v * PH : (v + 1) * PH, :])
        for v in range(NV)
    ]
    for u in range(NV):
        turned = 0.1 * sum(jac_ref[2, u, v] * side[v] for v in range(NV))
        add_ref[u, 2 * RAD : 2 * RAD + PH, :] = packed * side[u] + jnp.where(
            even_lane, turned, -turned
        )
    for last in range(2):
        at = 2 * PH + last * RAD
        near = 0.2 * near_ref[at : at + RAD, :]
        ends = []
        for v in range(NV):
            a, b = lon_a_ref[v * RAD : (v + 1) * RAD, :], lon_b_ref[v * RAD : (v + 1) * RAD, :]
            ends.append(jnp.where(odd, b, a) if last else jnp.where(odd, a, b))
        for u in range(NV):
            turned = 0.1 * sum(jac_ref[1, u, v] * ends[v] for v in range(NV))
            add_ref[u, last * RAD : (last + 1) * RAD, :] = near * ends[u] + (
                -turned if last else turned
            )
    keep = go(add_ref.at[NV // 2 :], keep_ref, sems.at[1])
    for u in range(NV // 2):
        loads[u].wait()
        corr = add_ref[u, 2 * RAD : 2 * RAD + PH, :]
        adds = [add_ref[u, last * RAD : (last + 1) * RAD, :] for last in range(2)]
        shell_edge_tile(u, x_ref, y_ref, o_ref, corr, adds, edge, sems.at[0])
    copy.wait()
    put_levels(cols_ref, level_ref, LEV)
    copy = go(level_ref, level_all, sems.at[2])
    wait_half(y_ref, 0, sems.at[0])
    keep.wait()
    copy.wait()


def shell_rest_kernel(half_ref, part_ref, keep_ref, o_ref, x_ref, y_ref, add_ref, part_sems, sems):
    keep = go(keep_ref, add_ref, sems.at[1])
    loads = load_part(part_ref, x_ref, part_sems, range(NV // 2, NV))
    edge = edge_of(PH)
    keep.wait()
    for u in range(NV // 2, NV):
        loads[u].wait()
        corr = add_ref[u - NV // 2, 2 * RAD : 2 * RAD + PH, :]
        adds = [add_ref[u - NV // 2, last * RAD : (last + 1) * RAD, :] for last in range(2)]
        shell_edge_tile(u, x_ref, y_ref, o_ref, corr, adds, edge, sems.at[0])
    wait_half(y_ref, 1, sems.at[0])


def pick_kernel(got_ref, where_ref, o_ref):
    where = where_ref[...]
    picked = jnp.zeros((PH, TH), F32)
    for b in range(BLOCKS):
        for s in range(2):
            picked = picked + jnp.where(where == float(2 * b + s), got_ref[b, s : s + 1, :], 0.0)
    o_ref[...] = picked


def call(kernel, name, ins, outs, specs, kept=(), scratch=(), flops=0, moved=0, aliases=None):
    ins = [
        pltpu.with_memory_space_constraint(x, pltpu.HBM) if spec is HBM else x
        for x, spec in zip(ins, specs)
    ]
    shapes = [
        pltpu.HBM(shape, F32) if i in kept else jax.ShapeDtypeStruct(shape, F32)
        for i, shape in enumerate(outs)
    ]
    places = [HBM if i in kept else VMEM for i in range(len(outs))]
    single = len(shapes) == 1
    return pl.pallas_call(
        kernel,
        out_shape=shapes[0] if single else shapes,
        in_specs=specs,
        out_specs=places[0] if single else places,
        scratch_shapes=list(scratch),
        compiler_params=PARAMS,
        input_output_aliases=aliases or {},
        cost_estimate=pl.CostEstimate(flops=flops, bytes_accessed=moved, transcendentals=0),
        name=name,
    )(*ins)


def swaps(count, first, periodic):
    pairs = []
    for i in range(first, count, 2):
        if i + 1 < count or periodic:
            j = (i + 1) % count
            pairs += [(i, j), (j, i)]
    return pairs


def exchange(lon_a, lon_b, lat):
    ring = ("comp", "lon")
    size = lax.axis_size("comp") * lax.axis_size("lon")
    width = lax.axis_size("lat")
    got_lat = [lax.ppermute(lat, "lat", swaps(width, first, False)) for first in (0, 1)]
    got_lon = [
        lax.ppermute(block, ring, swaps(size, first, True))
        for first, block in enumerate((lon_a, lon_b))
    ]
    return (*got_lon, *got_lat)


def shards(
    shell,
    resistivity,
    jacobians,
    current_weights,
    footpoint,
    footrow,
    slab,
    conductance,
    chemistry,
    coupling,
    potential_weights,
):
    coupling = coupling.T
    slab_scratch = pltpu.VMEM((LON, KF, TH), F32)
    shell_scratch = pltpu.VMEM(shell.shape, F32)
    flat_scratch = pltpu.VMEM((SHELL_ROWS * PH, TH), F32)

    def rows(count):
        return pltpu.VMEM((count, TH), F32)

    lon_a, lon_b, lat = call(
        pack_kernel,
        "pack",
        (slab, shell.reshape(SHELL_ROWS * PH, TH)),
        [(KF + SHELL_ROWS, TH), (KF + SHELL_ROWS, TH), (2 * NF + NV * PH, TH)],
        [HBM, HBM],
        scratch=[
            slab_scratch,
            flat_scratch,
            DMA((LEV,)),
            DMA((NV,)),
        ],
        moved=8_000_000,
    )
    halos = exchange(lon_a, lon_b, lat)
    middle, part, first, near = call(
        interior_kernel,
        "interior",
        (slab, shell, resistivity.reshape(RAD * PH, TH), jacobians, conductance, chemistry),
        [(LON, KF, TH), shell.shape, (NV, PH, TH), (2 * PH + 2 * RAD, TH)],
        [HBM, HBM, HBM, VMEM, VMEM, VMEM],
        kept=(1,),
        scratch=[
            slab_scratch,
            shell_scratch,
            shell_scratch,
            rows(RAD * PH),
            DMA((4,)),
        ],
        flops=90_000_000,
        moved=20_000_000,
    )
    send, where = call(
        current_kernel,
        "current",
        (first, near, jacobians, current_weights, footpoint, footrow, *halos),
        [(BLOCKS, 8, TH), (PH, TH)],
        [VMEM, VMEM, SMEM, SMEM, SMEM, SMEM] + [VMEM] * 4,
        scratch=[rows(PH), pltpu.SMEM((BLOCKS,), jnp.int32)],
    )
    got = lax.all_to_all(send, "lon", split_axis=0, concat_axis=0, tiled=True)
    part = part.reshape(SHELL_ROWS * PH, TH)
    shell_next, keep, levels = call(
        shell_edge_kernel,
        "shell_edge",
        (part, near, jacobians, *halos, coupling),
        [(SHELL_ROWS * PH, TH), (NV // 2, 2 * RAD + PH, TH), (KF, TH)],
        [HBM, VMEM, SMEM] + [VMEM] * 4 + [HBM],
        kept=(0, 1, 2),
        scratch=[
            flat_scratch,
            flat_scratch,
            pltpu.VMEM((NV, 2 * RAD + PH, TH), F32),
            pltpu.VMEM((LEV, NF), F32),
            rows(KF),
            DMA((NV,)),
            DMA((3,)),
        ],
        flops=10_000_000,
        moved=8_000_000,
    )
    got, shell_next, levels = lax.optimization_barrier((got, shell_next, levels))
    edges = [rows(2 * NF), pltpu.VMEM((2, KF, TH), F32)]
    middle, source, lon_a, lon_b, lat = call(
        middle_kernel,
        "middle",
        (middle, *halos, conductance, levels, got),
        [(LON, KF, TH), (LON, TH), (KF, TH), (KF, TH), (2 * NF, TH)],
        [VMEM] * 6 + [HBM, VMEM],
        scratch=[rows(KF), *edges, DMA],
        moved=8_000_000,
    )
    ends = exchange(lon_a, lon_b, lat)
    last, levels = call(
        second_kernel,
        "second",
        (middle, conductance, chemistry, coupling, potential_weights.reshape(1, NF)),
        [(LON, KF, TH), (KF + NF, TH)],
        [VMEM] * 3 + [HBM] * 2,
        scratch=[pltpu.VMEM((LEV, NF), F32), pltpu.VMEM((1, NF), F32), DMA((2,))],
        flops=60_000_000,
        moved=10_000_000,
    )
    asked = call(
        potential_kernel,
        "potential",
        (last, *ends, conductance, levels, source, got),
        [(BLOCKS, 8, TH)],
        [VMEM] * 9,
        scratch=[rows(LON), rows(NF), pltpu.VMEM((2, NF, TH), F32)],
    )
    asked, shell_next = lax.optimization_barrier((asked, shell_next))
    back = lax.all_to_all(asked, "lon", split_axis=0, concat_axis=0, tiled=True)
    slab_next = call(
        finish_kernel,
        "finish",
        (last, *ends, conductance, levels, source),
        [slab.shape],
        [VMEM] * 8,
        kept=(0,),
        scratch=[slab_scratch, *edges, DMA],
        moved=8_000_000,
    )
    shell_next = call(
        shell_rest_kernel,
        "shell_rest",
        (shell_next, part, keep),
        [(SHELL_ROWS * PH, TH)],
        [HBM] * 3,
        kept=(0,),
        scratch=[
            flat_scratch,
            flat_scratch,
            pltpu.VMEM((NV // 2, 2 * RAD + PH, TH), F32),
            DMA((NV,)),
            DMA((2,)),
        ],
        flops=10_000_000,
        moved=8_000_000,
        aliases={0: 0},
    ).reshape(shell.shape)
    boundary = call(pick_kernel, "pick", (back, where), [(PH, TH)], [VMEM] * 2)
    return shell_next, slab_next, boundary


def solution(mesh):
    ring = ("comp", "lon")
    placed = (
        P(None, None, ring, "lat"),
        P(None, ring, "lat"),
        P(),
        P(),
        P("lat", ring, None),
        P("lat", ring),
        P(None, None, ring, "lat"),
        P(ring, "lat"),
        P(),
        P(),
        P(),
    )
    return jax.shard_map(
        shards,
        mesh=mesh,
        in_specs=placed,
        out_specs=(P(None, None, ring, "lat"), P(None, None, ring, "lat"), P(ring, "lat")),
        check_vma=False,
    )
```

```python
import functools

import jax
import jax.numpy as jnp
from jax import lax
from jax.experimental import pallas as pl
from jax.experimental.pallas import tpu as pltpu
from jax.sharding import PartitionSpec as P

NV = 8
NF = 40
RAD = 32
PH = 16
TH = 128
LEV = 8
LON = 16
BLOCKS = 16
KF = LEV * NF
SHELL_ROWS = NV * RAD
F32 = jnp.float32
BF16 = jnp.bfloat16
VMEM = pl.BlockSpec(memory_space=pltpu.VMEM)
SMEM = pl.BlockSpec(memory_space=pltpu.SMEM)
HBM = pl.BlockSpec(memory_space=pltpu.HBM)
DMA = pltpu.SemaphoreType.DMA
PARAMS = pltpu.CompilerParams(vmem_limit_bytes=24 * 1024 * 1024)


def go(source, target, sem):
    copy = pltpu.make_async_copy(source, target, sem)
    copy.start()
    return copy


def odd_lon():
    return lax.rem(lax.axis_index("lon"), 2) == 1


def odd_lat():
    return lax.rem(lax.axis_index("lat"), 2) == 1


def lanes(rows):
    return lax.broadcasted_iota(jnp.int32, (rows, TH), 1)


def slot_of(rows):
    return lax.rem(lanes(rows) + 1, TH) // 2


def edge_of(rows):
    lane = lanes(rows)
    return (lane == 0) | (lane == TH - 1)


def spin(x, shift):
    shift = shift % TH
    return x if shift == 0 else pltpu.roll(x, shift, 1)


def merged(first, second):
    odd = odd_lat()
    left = jnp.where(odd, first, second)
    right = jnp.where(odd, second, first)
    even_lane = lax.rem(lanes(left.shape[0]), 2) == 0
    return jnp.where(even_lane, spin(left, 1), spin(right, -1))


def load_level(slab_ref, s2_ref, sem, k):
    for l in range(LON):
        go(slab_ref.at[:, k, l, :], s2_ref.at[l, k * NF : (k + 1) * NF, :], sem)


def level_rows(ref, k):
    return ref.at[:, k * NF : (k + 1) * NF, :]


def wait_level(s2_ref, sems, k):
    part = level_rows(s2_ref, k)
    pltpu.make_async_copy(part, part, sems.at[k]).wait()


def pack_level(s2_ref, k, slot, acc):
    for l in range(LON):
        j = l + LON * (k % 4)
        acc = jnp.where(slot == j, spin(s2_ref[l, k * NF : (k + 1) * NF, :], 2 * j), acc)
    return acc


def pack_kernel(
    slab_ref, shell_ref, lon_a_ref, lon_b_ref, lat_ref,
    s2_ref, sh_ref, slab_sems, shell_sems,
):
    copies = [
        go(
            shell_ref.at[v * RAD * PH : (v + 1) * RAD * PH],
            sh_ref.at[v * RAD * PH : (v + 1) * RAD * PH],
            shell_sems.at[v],
        )
        for v in range(NV)
    ]
    odd = odd_lon()
    slot = slot_of(PH)
    for v in range(NV):
        load_level(slab_ref, s2_ref, slab_sems.at[v], v)
        copies[v].wait()
        acc = jnp.zeros((PH, TH), F32)
        for r in range(RAD):
            x = sh_ref[(v * RAD + r) * PH : (v * RAD + r + 1) * PH, :]
            acc = jnp.where(slot == r, spin(x, 2 * r), acc)
        lat_ref[2 * NF + v * PH : 2 * NF + (v + 1) * PH, :] = acc
        low = sh_ref[pl.ds(v * RAD * PH, RAD, stride=PH), :]
        high = sh_ref[pl.ds(v * RAD * PH + PH - 1, RAD, stride=PH), :]
        at = KF + v * RAD
        lon_a_ref[at : at + RAD, :] = jnp.where(odd, low, high)
        lon_b_ref[at : at + RAD, :] = jnp.where(odd, high, low)
    slot = slot_of(NF)
    for half in range(2):
        acc = jnp.zeros((NF, TH), F32)
        for k in range(4 * half, 4 * half + 4):
            wait_level(s2_ref, slab_sems, k)
            acc = pack_level(s2_ref, k, slot, acc)
        lat_ref[half * NF : (half + 1) * NF, :] = acc
    low, high = s2_ref[0], s2_ref[LON - 1]
    lon_a_ref[0:KF, :] = jnp.where(odd, low, high)
    lon_b_ref[0:KF, :] = jnp.where(odd, high, low)


def mixing_matrix(chem):
    rows = (lax.broadcasted_iota(jnp.int32, (2 * NF, NF), 0) % NF) == lax.broadcasted_iota(
        jnp.int32, (2 * NF, NF), 1
    )
    cols = lax.broadcasted_iota(jnp.int32, (NF, 6 * NF), 0) == (
        lax.broadcasted_iota(jnp.int32, (NF, 6 * NF), 1) % NF
    )
    wide = jnp.dot(
        jnp.dot(
            rows.astype(F32), chem, precision=lax.Precision.HIGHEST, preferred_element_type=F32
        ),
        cols.astype(F32),
        precision=lax.Precision.HIGHEST,
        preferred_element_type=F32,
    )
    i = lax.broadcasted_iota(jnp.int32, (2 * NF, 6 * NF), 0)
    j = lax.broadcasted_iota(jnp.int32, (2 * NF, 6 * NF), 1)
    wide = jnp.where((i // NF) == ((j // NF) % 2), 0.1 * wide, 0.0)
    high = wide.astype(BF16).astype(F32)
    return jnp.where(j < 4 * NF, high, wide - high).astype(BF16)


def step(x_ref, cond_ref, chem_ref, o_ref):
    lhs = mixing_matrix(chem_ref[...])
    lane = lanes(2 * NF)
    zero = jnp.zeros((NF, TH), F32)

    def body(g, carry):
        for kp in range(LEV // 2):
            rows = slice(2 * NF * kp, 2 * NF * (kp + 1))
            xs = [x_ref[2 * g, rows, :], x_ref[2 * g + 1, rows, :]]
            below = x_ref[jnp.maximum(2 * g - 1, 0), rows, :] * jnp.where(g > 0, 1.0, 0.0)
            above = x_ref[jnp.minimum(2 * g + 2, LON - 1), rows, :] * jnp.where(
                g < LON // 2 - 1, 1.0, 0.0
            )
            near = [below + xs[1], xs[0] + above]
            both = jnp.concatenate(xs, axis=1)
            high = both.astype(BF16)
            low = (both - high.astype(F32)).astype(BF16)
            mixed = jnp.dot(
                lhs, jnp.concatenate([high, low, high], axis=0), preferred_element_type=F32
            )
            for i in range(2):
                x = xs[i]
                l = 2 * g + i
                if kp == 0:
                    down = jnp.concatenate([zero, x[:NF]], axis=0)
                else:
                    down = x_ref[l, 2 * NF * kp - NF : 2 * NF * kp + NF, :]
                if kp == LEV // 2 - 1:
                    up = jnp.concatenate([x[NF:], zero], axis=0)
                else:
                    up = x_ref[l, 2 * NF * kp + NF : 2 * NF * kp + 3 * NF, :]
                sides = jnp.where(lane == 0, 0.0, spin(x, 1)) + jnp.where(
                    lane == TH - 1, 0.0, spin(x, -1)
                )
                c = 0.1 * cond_ref[pl.ds(l, 1), :]
                o_ref[l, rows, :] = (
                    x * (0.8 - 4.0 * c)
                    + c * (near[i] + sides)
                    + 0.1 * (up + down)
                    + mixed[:, i * TH : (i + 1) * TH]
                )
        return carry

    lax.fori_loop(0, LON // 2, body, 0, unroll=4)


def shell_matrices(jac_ref):
    size = NV * PH
    spread = (
        lax.broadcasted_iota(jnp.int32, (size, NV), 0) // PH
        == lax.broadcasted_iota(jnp.int32, (size, NV), 1)
    ).astype(F32)
    columns = lax.broadcasted_iota(jnp.int32, (3 * NV, 3 * size), 1)
    gather = (lax.broadcasted_iota(jnp.int32, (3 * NV, 3 * size), 0) == columns // PH).astype(F32)
    i = lax.broadcasted_iota(jnp.int32, (size, size), 0)
    j = lax.broadcasted_iota(jnp.int32, (size, size), 1)
    apart = (j % PH) - (i % PH)
    exact = dict(precision=lax.Precision.HIGHEST, preferred_element_type=F32)
    three = jnp.concatenate([jac_ref[d] for d in range(3)], axis=1)
    spread_out = 0.1 * jnp.dot(jnp.dot(spread, three, **exact), gather, **exact)

    def wide(d):
        return spread_out[:, d * size : (d + 1) * size]

    turn = wide(1)
    parts = [
        jnp.where(apart == 1, turn, jnp.where(apart == -1, -turn, 0.0)),
        jnp.where(apart == 0, wide(0), 0.0),
        jnp.where(apart == 0, wide(2), 0.0),
    ]
    high = [part.astype(BF16) for part in parts]
    low = [(part - h.astype(F32)).astype(BF16) for part, h in zip(parts, high)]
    same = (i // PH) == (j // PH)
    sums = jnp.where(same & ((apart == 1) | (apart == -1)), 1.0, 0.0).astype(BF16)
    return jnp.concatenate(high + high + low, axis=1), jnp.concatenate([sums, sums], axis=1)


def halves(x):
    high = x.astype(BF16)
    return high, (x - high.astype(F32)).astype(BF16)


def shell_part(x_ref, res_ref, jac_ref, o_ref, done):
    flux_of, sums_of = shell_matrices(jac_ref)
    lane = lanes(NV * PH)

    def rows_of(r):
        return jnp.concatenate([x_ref[v, r] for v in range(NV)], axis=0)

    def body(g, carry):
        r = 2 * g
        below = rows_of(jnp.maximum(r - 1, 0)) * jnp.where(g > 0, 1.0, 0.0)
        x = [rows_of(r), rows_of(r + 1)]
        above = rows_of(jnp.minimum(r + 2, RAD - 1)) * jnp.where(g < RAD // 2 - 1, 1.0, 0.0)
        radial = jnp.concatenate([x[1] - below, above - x[0]], axis=1)
        south = [jnp.where(lane == 0, 0.0, spin(a, 1)) for a in x]
        north = [jnp.where(lane == TH - 1, 0.0, spin(a, -1)) for a in x]
        polar = jnp.concatenate([n - s for n, s in zip(north, south)], axis=1)
        xh, xl = halves(jnp.concatenate(x, axis=1))
        rh, rl = halves(radial)
        ph, pl_ = halves(polar)
        flux = jnp.dot(
            flux_of,
            jnp.concatenate([xh, rh, ph, xl, rl, pl_, xh, rh, ph], axis=0),
            preferred_element_type=F32,
        )
        sums = jnp.dot(
            sums_of, jnp.concatenate([xh, xl], axis=0), preferred_element_type=F32
        )
        around = [below + x[1], x[0] + above]
        for i in range(2):
            at = slice(i * TH, (i + 1) * TH)
            lap = (around[i] + sums[:, at]) + (south[i] + north[i]) - 6.0 * x[i]
            res = 0.2 * res_ref[pl.ds(pl.multiple_of((r + i) * PH, PH), PH), :]
            for v in range(NV):
                rows = slice(v * PH, (v + 1) * PH)
                o_ref[v, r + i] = x[i][rows] + res * lap[rows] - flux[rows, at]
        done(r)
        return carry

    lax.fori_loop(0, RAD // 2, body, 0, unroll=4)


def interior_kernel(
    slab_ref, shell_ref, res_ref, jac_ref, cond_ref, chem_ref, coupling_ref,
    m_ref, part_ref, first_ref, near_ref,
    s2_ref, sh_ref, so_ref, rs_ref, sems,
):
    one = go(shell_ref, sh_ref, sems.at[0])
    two = go(res_ref, rs_ref, sems.at[1])
    for k in range(LEV):
        load_level(slab_ref, s2_ref, sems.at[3], k)
    two.wait()
    slot = slot_of(PH)
    packed = jnp.zeros((PH, TH), F32)
    for r in range(RAD):
        packed = jnp.where(slot == r, spin(rs_ref[r * PH : (r + 1) * PH, :], 2 * r), packed)
    near_ref[0:PH, :] = rs_ref[0:PH, :]
    near_ref[PH : 2 * PH, :] = packed
    for last in range(2):
        at = 2 * PH + last * RAD
        near_ref[at : at + RAD, :] = rs_ref[pl.ds(last * (PH - 1), RAD, stride=PH), :]
    one.wait()

    def send_shell(r):
        go(so_ref.at[:, pl.ds(r, 2)], part_ref.at[:, pl.ds(r, 2)], sems.at[2])

    shell_part(sh_ref, rs_ref, jac_ref, so_ref, send_shell)
    first_ref[...] = so_ref[:, 0]
    pltpu.make_async_copy(s2_ref, s2_ref, sems.at[3]).wait()
    step(s2_ref, cond_ref, chem_ref, m_ref)
    pltpu.make_async_copy(so_ref, part_ref, sems.at[2]).wait()


def rank_rows(fp_ref, count_ref, visit):
    for b in range(BLOCKS):
        count_ref[b] = 0
    for p in range(PH):
        block = fp_ref[0, p, 0]
        rank = count_ref[block]
        count_ref[block] = rank + 1
        visit(p, block, rank)


def current_kernel(
    part_ref, res_all_ref, jac_ref, weight_ref, fp_ref, row_ref, lon_a_all, lon_b_all, lat_a_all, lat_b_all,
    send_ref, where_ref, cur_ref, count_ref,
):
    lon_a_ref, lon_b_ref = lon_a_all.at[KF:, :], lon_b_all.at[KF:, :]
    lat_a_ref, lat_b_ref = lat_a_all.at[2 * NF :, :], lat_b_all.at[2 * NF :, :]
    send_ref[...] = jnp.zeros(send_ref.shape, F32)
    w = [weight_ref[v] for v in range(NV)]
    wj = [[sum(w[u] * jac_ref[d, u, v] for u in range(NV)) for v in range(NV)] for d in (1, 2)]
    odd = odd_lon()
    cur = sum(w[v] * part_ref[v] for v in range(NV))
    res = 0.2 * res_all_ref[0:PH, :]
    rows_a = [lon_a_ref[v * RAD : v * RAD + 1, :] for v in range(NV)]
    rows_b = [lon_b_ref[v * RAD : v * RAD + 1, :] for v in range(NV)]
    low = [jnp.where(odd, a, b) for a, b in zip(rows_a, rows_b)]
    high = [jnp.where(odd, b, a) for a, b in zip(rows_a, rows_b)]
    row = lax.broadcasted_iota(jnp.int32, (PH, TH), 0)
    lane = lanes(PH)
    plain = sum(w[v] * low[v] for v in range(NV))
    turned = 0.1 * sum(wj[0][v] * low[v] for v in range(NV))
    cur = cur + jnp.where(row == 0, res * plain + turned, 0.0)
    plain = sum(w[v] * high[v] for v in range(NV))
    turned = 0.1 * sum(wj[0][v] * high[v] for v in range(NV))
    cur = cur + jnp.where(row == PH - 1, res * plain - turned, 0.0)
    side = [
        merged(
            lat_a_ref[v * PH : (v + 1) * PH, :],
            lat_b_ref[v * PH : (v + 1) * PH, :],
        )
        for v in range(NV)
    ]
    plain = sum(w[v] * side[v] for v in range(NV))
    turned = 0.1 * sum(wj[1][v] * side[v] for v in range(NV))
    cur = cur + jnp.where(lane == 0, res * plain + turned, 0.0)
    cur = cur + jnp.where(lane == TH - 1, res * plain - turned, 0.0)
    cur_ref[...] = cur

    def visit(p, block, rank):
        where_ref[p : p + 1, :] = jnp.full((1, TH), 2 * block + rank, jnp.int32).astype(F32)
        send_ref[block, pl.ds(rank, 1), :] = cur_ref[p : p + 1, :]
        send_ref[block, pl.ds(2 + rank, 1), :] = jnp.full((1, TH), row_ref[0, p], jnp.int32).astype(F32)

    rank_rows(fp_ref, count_ref, visit)


def slab_edges(lat_a, lat_b):
    return [
        merged(lat_a[h * NF : (h + 1) * NF, :], lat_b[h * NF : (h + 1) * NF, :]) for h in range(2)
    ]


def column(row):
    diagonal = lax.broadcasted_iota(jnp.int32, (NF, NF), 0) == lax.broadcasted_iota(
        jnp.int32, (NF, NF), 1
    )
    return jnp.broadcast_to(
        jnp.sum(
            jnp.where(diagonal, jnp.broadcast_to(row, (NF, NF)), 0.0), axis=1, keepdims=True
        ),
        (NF, TH),
    )


def put_levels(coupling_ref, level_ref, count):
    for k in range(count):
        level_ref[k * NF : (k + 1) * NF, :] = column(0.1 * coupling_ref[k : k + 1, :])


def gather_source(got_ref):
    row = lax.broadcasted_iota(jnp.int32, (LON, TH), 0).astype(F32)
    source = jnp.zeros((LON, TH), F32)
    for b in range(BLOCKS):
        for s in range(2):
            source = source + jnp.where(
                row == got_ref[b, 2 + s : 3 + s, :], got_ref[b, s : s + 1, :], 0.0
            )
    return source


def fixed_tile(x, l, k, c, edge, side_ref, level_ref, source, end_ref):
    rows = slice(k * NF, (k + 1) * NF)
    j = l + LON * (k % 4)
    h = jnp.where(edge, spin(side_ref[(k // 4) * NF : (k // 4 + 1) * NF, :], -2 * j), 0.0)
    if l == 0:
        h = h + end_ref[0, rows, :]
    if l == LON - 1:
        h = h + end_ref[1, rows, :]
    return x + c * h + level_ref[rows, :] * source


def put_edges(lon_a_ref, lon_b_ref, lat_a_ref, lat_b_ref, side_ref, end_ref):
    odd = odd_lon()
    a, b = lon_a_ref[...], lon_b_ref[...]
    end_ref[0] = jnp.where(odd, a, b)
    end_ref[1] = jnp.where(odd, b, a)
    for at in range(0, side_ref.shape[0], NF):
        side_ref[at : at + NF, :] = merged(lat_a_ref[at : at + NF, :], lat_b_ref[at : at + NF, :])


def middle_kernel(
    x_ref, lon_a_all, lon_b_all, lat_a_all, lat_b_all, cond_ref, coupling_ref, got_ref,
    o_ref, source_ref, next_a_ref, next_b_ref, lat_ref,
    level_ref, side_ref, end_ref,
):
    put_levels(coupling_ref, level_ref, LEV)
    lon_a_ref, lon_b_ref = lon_a_all.at[0:KF, :], lon_b_all.at[0:KF, :]
    lat_a_ref, lat_b_ref = lat_a_all.at[0 : 2 * NF, :], lat_b_all.at[0 : 2 * NF, :]
    source_ref[...] = gather_source(got_ref)
    put_edges(lon_a_ref, lon_b_ref, lat_a_ref, lat_b_ref, side_ref, end_ref)
    edge = edge_of(NF)
    slot = slot_of(NF)
    for l in range(LON):
        c = 0.1 * cond_ref[l : l + 1, :]
        source = source_ref[l : l + 1, :]
        for k in range(LEV):
            rows = slice(k * NF, (k + 1) * NF)
            x = fixed_tile(x_ref[l, rows, :], l, k, c, edge, side_ref, level_ref, source, end_ref)
            o_ref[l, rows, :] = x
    for half in range(2):
        acc = jnp.zeros((NF, TH), F32)
        for k in range(4 * half, 4 * half + 4):
            acc = pack_level(o_ref, k, slot, acc)
        lat_ref[half * NF : (half + 1) * NF, :] = acc
    odd = odd_lon()
    low, high = o_ref[0], o_ref[LON - 1]
    next_a_ref[...] = jnp.where(odd, low, high)
    next_b_ref[...] = jnp.where(odd, high, low)


def second_kernel(
    x_ref, cond_ref, chem_ref, coupling_ref, weight_ref, m_ref, level_ref, near_ref, last_ref, sems
):
    copies = [go(coupling_ref, near_ref, sems.at[0]), go(weight_ref, last_ref, sems.at[1])]
    step(x_ref, cond_ref, chem_ref, m_ref)
    for copy in copies:
        copy.wait()
    put_levels(near_ref, level_ref, LEV)
    level_ref[KF : KF + NF, :] = column(last_ref[...])


def potential_kernel(
    x_ref, lon_a_all, lon_b_all, lat_a_all, lat_b_all, cond_ref, level_ref, source_ref, got_ref,
    send_ref,
    pot_ref, side_ref, end_ref,
):
    lon_a_ref, lon_b_ref = lon_a_all.at[0:NF, :], lon_b_all.at[0:NF, :]
    lat_a_ref, lat_b_ref = lat_a_all.at[0:NF, :], lat_b_all.at[0:NF, :]
    edge = edge_of(NF)
    weight = level_ref[KF : KF + NF, :]
    put_edges(lon_a_ref, lon_b_ref, lat_a_ref, lat_b_ref, side_ref, end_ref)
    for l in range(LON):
        c = 0.1 * cond_ref[l : l + 1, :]
        x = fixed_tile(
            x_ref[l, 0:NF, :], l, 0, c, edge, side_ref, level_ref, source_ref[l : l + 1, :], end_ref
        )
        pot_ref[l : l + 1, :] = jnp.sum(weight * x, axis=0, keepdims=True)
    potential = pot_ref[...]
    row = lax.broadcasted_iota(jnp.int32, (LON, TH), 0).astype(F32)
    for b in range(BLOCKS):
        for s in range(2):
            send_ref[b, s : s + 1, :] = jnp.sum(
                jnp.where(row == got_ref[b, 2 + s : 3 + s, :], potential, 0.0), axis=0, keepdims=True
            )
        send_ref[b, 2:8, :] = jnp.zeros((6, TH), F32)


def finish_kernel(
    x_ref, lon_a_ref, lon_b_ref, lat_a_ref, lat_b_ref, cond_ref, level_ref, source_ref,
    o_ref,
    y_ref, side_ref, end_ref, sem,
):
    edge = edge_of(NF)
    put_edges(lon_a_ref, lon_b_ref, lat_a_ref, lat_b_ref, side_ref, end_ref)
    for l in range(LON):
        c = 0.1 * cond_ref[l : l + 1, :]
        source = source_ref[l : l + 1, :]
        for k in range(LEV):
            rows = slice(k * NF, (k + 1) * NF)
            y_ref[l, rows, :] = fixed_tile(
                x_ref[l, rows, :], l, k, c, edge, side_ref, level_ref, source, end_ref
            )
            go(y_ref.at[l, rows, :], o_ref.at[:, k, l, :], sem)
    pltpu.make_async_copy(y_ref, y_ref, sem).wait()


def shell_edge_tile(u, x_ref, y_ref, o_ref, corr, adds, edge, sem):
    size = RAD * PH
    for r in range(RAD):
        rows = slice((u * RAD + r) * PH, (u * RAD + r + 1) * PH)
        y_ref[rows, :] = x_ref[rows, :] + jnp.where(edge, spin(corr, -2 * r), 0.0)
    for last in range(2):
        where = pl.ds(u * size + last * (PH - 1), RAD, stride=PH)
        y_ref[where, :] = y_ref[where, :] + adds[last]
    go(y_ref.at[u * size : (u + 1) * size], o_ref.at[u * size : (u + 1) * size], sem)


def load_part(part_ref, x_ref, part_sems, these):
    size = RAD * PH
    return {
        u: go(
            part_ref.at[u * size : (u + 1) * size], x_ref.at[u * size : (u + 1) * size], part_sems.at[u]
        )
        for u in these
    }


def wait_half(y_ref, first, sem):
    half = NV // 2 * RAD * PH
    part = y_ref.at[first * half : (first + 1) * half]
    pltpu.make_async_copy(part, part, sem).wait()


def shell_edge_kernel(
    part_ref, near_ref, jac_ref, lon_a_all, lon_b_all, lat_a_all, lat_b_all,
    o_ref, keep_ref,
    x_ref, y_ref, add_ref, part_sems, sems,
):
    loads = load_part(part_ref, x_ref, part_sems, range(NV // 2))
    lon_a_ref, lon_b_ref = lon_a_all.at[KF:, :], lon_b_all.at[KF:, :]
    lat_a_ref, lat_b_ref = lat_a_all.at[2 * NF :, :], lat_b_all.at[2 * NF :, :]
    odd = odd_lon()
    edge = edge_of(PH)
    even_lane = lax.rem(lanes(PH), 2) == 0
    packed = 0.2 * near_ref[PH : 2 * PH, :]
    side = [
        merged(lat_a_ref[v * PH : (v + 1) * PH, :], lat_b_ref[v * PH : (v + 1) * PH, :])
        for v in range(NV)
    ]
    for u in range(NV):
        turned = 0.1 * sum(jac_ref[2, u, v] * side[v] for v in range(NV))
        add_ref[u, 2 * RAD : 2 * RAD + PH, :] = packed * side[u] + jnp.where(
            even_lane, turned, -turned
        )
    for last in range(2):
        at = 2 * PH + last * RAD
        near = 0.2 * near_ref[at : at + RAD, :]
        ends = []
        for v in range(NV):
            a, b = lon_a_ref[v * RAD : (v + 1) * RAD, :], lon_b_ref[v * RAD : (v + 1) * RAD, :]
            ends.append(jnp.where(odd, b, a) if last else jnp.where(odd, a, b))
        for u in range(NV):
            turned = 0.1 * sum(jac_ref[1, u, v] * ends[v] for v in range(NV))
            add_ref[u, last * RAD : (last + 1) * RAD, :] = near * ends[u] + (
                -turned if last else turned
            )
    keep = go(add_ref.at[NV // 2 :], keep_ref, sems.at[1])
    for u in range(NV // 2):
        loads[u].wait()
        corr = add_ref[u, 2 * RAD : 2 * RAD + PH, :]
        adds = [add_ref[u, last * RAD : (last + 1) * RAD, :] for last in range(2)]
        shell_edge_tile(u, x_ref, y_ref, o_ref, corr, adds, edge, sems.at[0])
    wait_half(y_ref, 0, sems.at[0])
    keep.wait()


def shell_rest_kernel(half_ref, part_ref, keep_ref, o_ref, x_ref, y_ref, add_ref, part_sems, sems):
    keep = go(keep_ref, add_ref, sems.at[1])
    loads = load_part(part_ref, x_ref, part_sems, range(NV // 2, NV))
    edge = edge_of(PH)
    keep.wait()
    for u in range(NV // 2, NV):
        loads[u].wait()
        corr = add_ref[u - NV // 2, 2 * RAD : 2 * RAD + PH, :]
        adds = [add_ref[u - NV // 2, last * RAD : (last + 1) * RAD, :] for last in range(2)]
        shell_edge_tile(u, x_ref, y_ref, o_ref, corr, adds, edge, sems.at[0])
    wait_half(y_ref, 1, sems.at[0])


def pick_kernel(got_ref, where_ref, o_ref):
    where = where_ref[...]
    picked = jnp.zeros((PH, TH), F32)
    for b in range(BLOCKS):
        for s in range(2):
            picked = picked + jnp.where(where == float(2 * b + s), got_ref[b, s : s + 1, :], 0.0)
    o_ref[...] = picked


def call(kernel, name, ins, outs, specs, kept=(), scratch=(), flops=0, moved=0, aliases=None):
    ins = [
        pltpu.with_memory_space_constraint(x, pltpu.HBM) if spec is HBM else x
        for x, spec in zip(ins, specs)
    ]
    shapes = [
        pltpu.HBM(shape, F32) if i in kept else jax.ShapeDtypeStruct(shape, F32)
        for i, shape in enumerate(outs)
    ]
    places = [HBM if i in kept else VMEM for i in range(len(outs))]
    single = len(shapes) == 1
    return pl.pallas_call(
        kernel,
        out_shape=shapes[0] if single else shapes,
        in_specs=specs,
        out_specs=places[0] if single else places,
        scratch_shapes=list(scratch),
        compiler_params=PARAMS,
        input_output_aliases=aliases or {},
        cost_estimate=pl.CostEstimate(flops=flops, bytes_accessed=moved, transcendentals=0),
        name=name,
    )(*ins)


def swaps(count, first, periodic):
    pairs = []
    for i in range(first, count, 2):
        if i + 1 < count or periodic:
            j = (i + 1) % count
            pairs += [(i, j), (j, i)]
    return pairs


def exchange(lon_a, lon_b, lat):
    ring = ("comp", "lon")
    size = lax.axis_size("comp") * lax.axis_size("lon")
    width = lax.axis_size("lat")
    got_lat = [lax.ppermute(lat, "lat", swaps(width, first, False)) for first in (0, 1)]
    got_lon = [
        lax.ppermute(block, ring, swaps(size, first, True))
        for first, block in enumerate((lon_a, lon_b))
    ]
    return (*got_lon, *got_lat)


def shards(
    shell,
    resistivity,
    jacobians,
    current_weights,
    footpoint,
    footrow,
    slab,
    conductance,
    chemistry,
    coupling,
    potential_weights,
):
    coupling = coupling.T
    slab_scratch = pltpu.VMEM((LON, KF, TH), F32)
    shell_scratch = pltpu.VMEM(shell.shape, F32)
    flat_scratch = pltpu.VMEM((SHELL_ROWS * PH, TH), F32)

    def rows(count):
        return pltpu.VMEM((count, TH), F32)

    lon_a, lon_b, lat = call(
        pack_kernel,
        "pack",
        (slab, shell.reshape(SHELL_ROWS * PH, TH)),
        [(KF + SHELL_ROWS, TH), (KF + SHELL_ROWS, TH), (2 * NF + NV * PH, TH)],
        [HBM, HBM],
        scratch=[
            slab_scratch,
            flat_scratch,
            DMA((LEV,)),
            DMA((NV,)),
        ],
        moved=8_000_000,
    )
    halos = exchange(lon_a, lon_b, lat)
    middle, part, first, near = call(
        interior_kernel,
        "interior",
        (slab, shell, resistivity.reshape(RAD * PH, TH), jacobians, conductance, chemistry, coupling),
        [(LON, KF, TH), shell.shape, (NV, PH, TH), (2 * PH + 2 * RAD, TH)],
        [HBM, HBM, HBM, VMEM, VMEM, VMEM, VMEM],
        kept=(1,),
        scratch=[
            slab_scratch,
            shell_scratch,
            shell_scratch,
            rows(RAD * PH),
            DMA((4,)),
        ],
        flops=90_000_000,
        moved=20_000_000,
    )
    send, where = call(
        current_kernel,
        "current",
        (first, near, jacobians, current_weights, footpoint, footrow, *halos),
        [(BLOCKS, 8, TH), (PH, TH)],
        [VMEM, VMEM, SMEM, SMEM, SMEM, SMEM] + [VMEM] * 4,
        scratch=[rows(PH), pltpu.SMEM((BLOCKS,), jnp.int32)],
    )
    got = lax.all_to_all(send, "lon", split_axis=0, concat_axis=0, tiled=True)
    part = part.reshape(SHELL_ROWS * PH, TH)
    shell_next, keep = call(
        shell_edge_kernel,
        "shell_edge",
        (part, near, jacobians, *halos),
        [(SHELL_ROWS * PH, TH), (NV // 2, 2 * RAD + PH, TH)],
        [HBM, VMEM, SMEM] + [VMEM] * 4,
        kept=(0, 1),
        scratch=[
            flat_scratch,
            flat_scratch,
            pltpu.VMEM((NV, 2 * RAD + PH, TH), F32),
            DMA((NV,)),
            DMA((2,)),
        ],
        flops=10_000_000,
        moved=8_000_000,
    )
    got, shell_next = lax.optimization_barrier((got, shell_next))
    edges = [rows(2 * NF), pltpu.VMEM((2, KF, TH), F32)]
    middle, source, lon_a, lon_b, lat = call(
        middle_kernel,
        "middle",
        (middle, *halos, conductance, coupling, got),
        [(LON, KF, TH), (LON, TH), (KF, TH), (KF, TH), (2 * NF, TH)],
        [VMEM] * 8,
        scratch=[rows(KF), *edges],
        moved=8_000_000,
    )
    ends = exchange(lon_a, lon_b, lat)
    last, levels = call(
        second_kernel,
        "second",
        (middle, conductance, chemistry, coupling, potential_weights.reshape(1, NF)),
        [(LON, KF, TH), (KF + NF, TH)],
        [VMEM] * 3 + [HBM] * 2,
        scratch=[pltpu.VMEM((LEV, NF), F32), pltpu.VMEM((1, NF), F32), DMA((2,))],
        flops=60_000_000,
        moved=10_000_000,
    )
    asked = call(
        potential_kernel,
        "potential",
        (last, *ends, conductance, levels, source, got),
        [(BLOCKS, 8, TH)],
        [VMEM] * 9,
        scratch=[rows(LON), rows(NF), pltpu.VMEM((2, NF, TH), F32)],
    )
    asked, shell_next = lax.optimization_barrier((asked, shell_next))
    back = lax.all_to_all(asked, "lon", split_axis=0, concat_axis=0, tiled=True)
    slab_next = call(
        finish_kernel,
        "finish",
        (last, *ends, conductance, levels, source),
        [slab.shape],
        [VMEM] * 8,
        kept=(0,),
        scratch=[slab_scratch, *edges, DMA],
        moved=8_000_000,
    )
    shell_next = call(
        shell_rest_kernel,
        "shell_rest",
        (shell_next, part, keep),
        [(SHELL_ROWS * PH, TH)],
        [HBM] * 3,
        kept=(0,),
        scratch=[
            flat_scratch,
            flat_scratch,
            pltpu.VMEM((NV // 2, 2 * RAD + PH, TH), F32),
            DMA((NV,)),
            DMA((2,)),
        ],
        flops=10_000_000,
        moved=8_000_000,
        aliases={0: 0},
    ).reshape(shell.shape)
    boundary = call(pick_kernel, "pick", (back, where), [(PH, TH)], [VMEM] * 2)
    return shell_next, slab_next, boundary


def solution(mesh):
    ring = ("comp", "lon")
    placed = (
        P(None, None, ring, "lat"),
        P(None, ring, "lat"),
        P(),
        P(),
        P("lat", ring, None),
        P("lat", ring),
        P(None, None, ring, "lat"),
        P(ring, "lat"),
        P(),
        P(),
        P(),
    )
    return jax.shard_map(
        shards,
        mesh=mesh,
        in_specs=placed,
        out_specs=(P(None, None, ring, "lat"), P(None, None, ring, "lat"), P(ring, "lat")),
        check_vma=False,
    )
```
